512 devices in a mesh: dom: 512 (over z, x, y, core).
Axes of the slice: x: 4, y: 4, z: 16, core: 2. Of those that a mesh axis runs over, the one named last changes fastest.
Arguments:
- features: bfloat16 [262144, 256], P('dom'), may hold values from -20 to 20, as said below
- w_self: bfloat16 [256, 256], replicated, may hold values from -0.375 to 0.375
- w_neigh: bfloat16 [256, 256], replicated, may hold values from -0.375 to 0.375
- neighbors: int32 [262144, 10], P('dom'), may hold values from 0 to 1663
- degree: int32 [262144], P('dom'), may hold values from 1 to 10
- boundary: int32 [512, 9, 128], P('dom'), may hold values from 0 to 511
- upstream: bfloat16 [262144, 256], P('dom'), may hold values from -6 to 6
Outputs:
- hidden: bfloat16 [262144, 256], P('dom')
- node_grad: bfloat16 [262144, 256], P('dom')
- weight_step: float32 [512, 256], replicated
The draws below stay inside these ranges and needn't reach their ends.
Inputs may be any that keep to these rules, and one draw needn't show every extreme that they name: `features`: feature values lie in the stated range.
All inputs are finite; a program needn't handle non-finite values.
Results may differ from the reference program's by a relative error of at most 0.006.
Values may be sent and summed in bfloat16 or wider, within the bound.
No kernel may reach another device: no remote copies, remote signals or barrier semaphores. Data moves between devices by JAX's collectives and lax.ppermute only.
A program may use at most 64 MiB of HBM per device.

```python
import jax
import jax.numpy as jnp
from jax import lax

D = 256
NODE_DEV = 512
BND = 128
DEG = 10
LEVELS = 9
NODES = 262144
N_DOM = 512


def draw_features(key, part):
    key = jax.random.fold_in(key, 11)
    key_values, key_columns = jax.random.split(key, 2)
    ramp = 3.0 ** (jnp.arange(D, dtype=jnp.float32) / D)
    column_scale = ramp * jnp.exp(jax.random.uniform(key_columns, (D,), jnp.float32, -0.5, 0.5))
    values = jax.random.truncated_normal(key_values, -4.0, 4.0, (NODES, D), jnp.float32)
    return (values * column_scale[None, :]).astype(jnp.bfloat16)


def set_ends(values, rng, least, top_value):
    longest = values.shape.index(max(values.shape))
    spots = []
    for shift in (0, 1):
        where = [jax.random.randint(jax.random.fold_in(rng, axis), (), 0, length) for axis, length in enumerate(values.shape)]
        where[longest] = (where[longest] + shift) % values.shape[longest]
        spots.append(tuple(where))
    return values.at[spots[0]].set(least).at[spots[1]].set(top_value)


def block_scale(stream_key, extent, cuts, low, largest):
    def one(axis_at, shards_of):
        draws = jax.random.uniform(jax.random.fold_in(jax.random.fold_in(stream_key, 6), axis_at), (shards_of,), jnp.float32, low / len(cuts), largest / len(cuts))
        return jnp.repeat(jnp.exp(draws), extent[axis_at] // shards_of).reshape((-1,) + (1,) * (len(extent) - axis_at - 1))

    loudness = one(*cuts[0])
    for cut in cuts[1:]:
        loudness = loudness * one(*cut)
    return loudness


def bell_draw(key, extent, scale, reach, shards=(), held_as=jnp.bfloat16):
    values = scale * jax.random.normal(key, extent, jnp.float32)
    if shards:
        values = values * block_scale(key, extent, shards, -0.22, 0.18)
    return jnp.clip(values, -reach, reach).astype(held_as)


def setup_inputs(seed: int = 0) -> dict:
    seeds = jax.random.split(jax.random.key(seed), 8)
    features = draw_features(jax.random.fold_in(seeds[7], 71), 0)
    w_self = bell_draw(seeds[1], (D, D), D ** -0.5, 0.375)
    w_neigh = bell_draw(seeds[2], (D, D), D ** -0.5, 0.375)
    neighbors = set_ends(jax.random.randint(seeds[3], (NODES, DEG), 0, NODE_DEV + LEVELS * BND), jax.random.fold_in(seeds[3], 1), 0, (NODE_DEV + LEVELS * BND) - 1).astype(jnp.int32)
    degree = set_ends(jax.random.randint(seeds[4], (NODES,), 1, DEG + 1), jax.random.fold_in(seeds[4], 1), 1, DEG).astype(jnp.int32)
    boundary = set_ends(jax.random.randint(seeds[5], (N_DOM, LEVELS, BND), 0, NODE_DEV), jax.random.fold_in(seeds[5], 1), 0, NODE_DEV - 1).astype(jnp.int32)
    upstream = bell_draw(seeds[6], (NODES, D), 1.0, 6.0, ((0, 512),))
    return dict(features=features, w_self=w_self, w_neigh=w_neigh, neighbors=neighbors, degree=degree, boundary=boundary, upstream=upstream)


epsilon = 1e-06

def aggregate(packed):
    block, remote, slot_index, degree_int = packed
    extended = jnp.concatenate([block, remote.reshape(LEVELS * BND, D)], axis=0)
    summed = jnp.zeros((NODE_DEV, D), jnp.float32)
    for slot in range(DEG):
        usable = (slot < degree_int)[:, None]
        summed = summed + jnp.where(usable, extended[slot_index[:, slot]].astype(jnp.float32), jnp.float32(0.0))
    return (summed / degree_int.astype(jnp.float32)[:, None]).astype(jnp.bfloat16)

def spread(packed):
    slot_share, slot_index, degree_int = packed
    ext_grad = jnp.zeros((NODE_DEV + LEVELS * BND, D), jnp.float32)
    for slot in range(DEG):
        usable = (slot < degree_int)[:, None]
        ext_grad = ext_grad.at[slot_index[:, slot]].add(jnp.where(usable, slot_share, jnp.float32(0.0)))
    return (ext_grad[:NODE_DEV], ext_grad[NODE_DEV:].reshape(LEVELS, BND, D))

def collect(packed):
    local_part, returned, chosen = packed
    return local_part.at[chosen.reshape(-1)].add(returned.reshape(LEVELS * BND, D))

def reference(features, w_self, w_neigh, neighbors, degree, boundary, upstream):
    blocks = features.reshape(N_DOM, NODE_DEV, D)
    device_ids = jnp.arange(N_DOM, dtype=jnp.int32)
    level_ids = jnp.arange(LEVELS, dtype=jnp.int32)
    partner = jnp.bitwise_xor(device_ids[:, None], jnp.left_shift(jnp.int32(1), level_ids)[None, :])
    sent = jax.vmap(lambda block, chosen: block[chosen])(blocks, boundary)
    received = sent[partner, level_ids[None, :]]
    slot_blocks = neighbors.reshape(N_DOM, NODE_DEV, DEG)
    degree_blocks = degree.reshape(N_DOM, NODE_DEV)
    agg = lax.map(aggregate, (blocks, received, slot_blocks, degree_blocks)).reshape(NODES, D)
    pre_sum = jnp.dot(features, w_self, preferred_element_type=jnp.float32) + jnp.dot(agg, w_neigh, preferred_element_type=jnp.float32)
    hidden = jax.nn.silu(pre_sum).astype(jnp.bfloat16)
    sigmoid_pre = jax.nn.sigmoid(pre_sum)
    pre_grad = (upstream.astype(jnp.float32) * sigmoid_pre * (1.0 + pre_sum * (1.0 - sigmoid_pre))).astype(jnp.bfloat16)
    grad_self = jnp.dot(features.T, pre_grad, preferred_element_type=jnp.float32)
    grad_neigh = jnp.dot(agg.T, pre_grad, preferred_element_type=jnp.float32)
    stacked = jnp.concatenate([grad_self, grad_neigh], axis=0)
    weight_step = stacked * lax.rsqrt(jnp.mean(stacked * stacked) + epsilon)
    slot_share = jnp.dot(pre_grad, w_neigh.T, preferred_element_type=jnp.float32) / degree.astype(jnp.float32)[:, None]
    local_part, remote_part = lax.map(spread, (slot_share.reshape(N_DOM, NODE_DEV, D), slot_blocks, degree_blocks))
    returned = remote_part[partner, level_ids[None, :]]
    gathered = lax.map(collect, (local_part, returned, boundary)).reshape(NODES, D)
    node_grad = (jnp.dot(pre_grad, w_self.T, preferred_element_type=jnp.float32) + gathered).astype(jnp.bfloat16)
    return (hidden, node_grad, weight_step)
```

```python
import jax
import jax.numpy as jnp
from jax import lax
from jax.experimental import pallas as pl
from jax.experimental.pallas import tpu as pltpu
from jax.sharding import PartitionSpec as P

epsilon = 1e-06
f32 = jnp.float32
bf16 = jnp.bfloat16
FAST_BITS = 5
VMEM_LIMIT = 48 * 1024 * 1024
TRANSPOSED_LHS = (((0,), (0,)), ((), ()))
TRANSPOSED_RHS = (((1,), (1,)), ((), ()))


def dot(a, b, dims=(((1,), (0,)), ((), ()))):
    return lax.dot_general(a, b, dims, preferred_element_type=f32)


def call(body, outs, cost, *args, scratch=()):
    flops, moved = cost
    return pl.pallas_call(
        body,
        out_shape=outs,
        scratch_shapes=scratch,
        compiler_params=pltpu.CompilerParams(vmem_limit_bytes=VMEM_LIMIT),
        cost_estimate=pl.CostEstimate(flops=flops, bytes_accessed=moved, transcendentals=0),
    )(*args)


def shape(dims, dtype):
    return jax.ShapeDtypeStruct(dims, dtype)


def one_hot_columns(rows, node_dev):
    k = rows.shape[1]
    ids = lax.broadcasted_iota(jnp.int32, (node_dev, k), 0)
    return jnp.where(ids == rows, f32(1.0), f32(0.0)).astype(bf16)


def send_body(boundary_ref, features_ref, *sent_refs):
    node_dev = features_ref.shape[0]
    features = features_ref[...]
    for level, sent_ref in enumerate(sent_refs):
        pick = one_hot_columns(boundary_ref[level : level + 1, :], node_dev)
        sent_ref[...] = dot(pick, features, TRANSPOSED_LHS).astype(bf16)


def count_body(neighbors_ref, degree_ref, counts_ref):
    slots, node_dev = neighbors_ref.shape
    degree = degree_ref[...]
    live = [
        jnp.where(degree > slot, neighbors_ref[slot : slot + 1, :], -1) for slot in range(slots)
    ]
    step = 16
    ids = lax.broadcasted_iota(jnp.int32, (step, node_dev), 0)

    def block(at, carry):
        start = pl.multiple_of(at * step, step)
        here = ids + start
        total = jnp.zeros((step, node_dev), f32)
        for row in live:
            total = total + jnp.where(here == row, f32(1.0), f32(0.0))
        counts_ref[pl.ds(start, step), :] = total.astype(bf16)
        return carry

    lax.fori_loop(0, counts_ref.shape[0] // step, block, 0)


def layer_body(levels, *refs):
    counts_ref, features_ref, degree_ref, upstream_ref, w_self_ref, w_neigh_ref = refs[:6]
    received = refs[6 : 6 + levels]
    hidden_ref, stacked_ref, local_ref = refs[6 + levels : 9 + levels]
    returned = refs[9 + levels : 9 + 2 * levels]
    extended_ref = refs[9 + 2 * levels]
    node_dev, width = features_ref.shape
    bnd = received[0].shape[0]
    extended_ref[:node_dev, :] = features_ref[...]
    for level in range(levels):
        start = node_dev + level * bnd
        extended_ref[start : start + bnd, :] = received[level][...]
    degree = degree_ref[...].astype(f32)
    degree = jnp.transpose(jnp.broadcast_to(degree, (128, node_dev)))
    degree = jnp.concatenate([degree] * (width // 128), axis=1)
    agg = (dot(counts_ref[...], extended_ref[...], TRANSPOSED_LHS) / degree).astype(bf16)
    features = features_ref[...]
    pre_sum = dot(features, w_self_ref[...]) + dot(agg, w_neigh_ref[...])
    sigmoid_pre = jax.nn.sigmoid(pre_sum)
    hidden_ref[...] = (pre_sum * sigmoid_pre).astype(bf16)
    pre_grad = (
        upstream_ref[...].astype(f32) * sigmoid_pre * (1.0 + pre_sum * (1.0 - sigmoid_pre))
    ).astype(bf16)
    stacked_ref[:width, :] = dot(features, pre_grad, TRANSPOSED_LHS)
    stacked_ref[width:, :] = dot(agg, pre_grad, TRANSPOSED_LHS)
    share = (dot(pre_grad, w_neigh_ref[...], TRANSPOSED_RHS) / degree).astype(bf16)
    for level in range(levels):
        start = node_dev + level * bnd
        returned[level][...] = dot(counts_ref[start : start + bnd, :], share).astype(bf16)
    local_ref[...] = dot(pre_grad, w_self_ref[...], TRANSPOSED_RHS) + dot(
        counts_ref[:node_dev, :], share
    )


def collect_body(boundary_ref, local_ref, *refs):
    returned, node_grad_ref = refs[:-1], refs[-1]
    node_dev = local_ref.shape[0]
    total = local_ref[...]
    for level, rows_ref in enumerate(returned):
        pick = one_hot_columns(boundary_ref[level : level + 1, :], node_dev)
        total = total + dot(pick, rows_ref[...])
    node_grad_ref[...] = total.astype(bf16)


def sum_and_repeat_body(parts_ref, out_ref):
    total = parts_ref[0].astype(f32)
    for part in range(1, parts_ref.shape[0]):
        total = total + parts_ref[part].astype(f32)
    out_ref[...] = jnp.broadcast_to(total.astype(out_ref.dtype)[None], out_ref.shape)


def normalize_body(total_ref, out_ref):
    total = total_ref[...].astype(f32)
    mean = jnp.sum(total * total) / total.size
    out_ref[...] = total * lax.rsqrt(jnp.full((1, total.shape[1]), mean + epsilon, f32))


def bit_groups(devices, bits):
    mask = sum(1 << b for b in bits)
    groups = {}
    for i in range(devices):
        groups.setdefault(i & ~mask, []).append(i)
    return list(groups.values())


def exchange(x, groups):
    return lax.all_to_all(x, "dom", 0, 0, axis_index_groups=groups, tiled=True)


def total_over_devices(stacked, devices):
    bits = devices.bit_length() - 1
    rows, width = stacked.shape
    near = bit_groups(devices, range(FAST_BITS))
    far = bit_groups(devices, range(FAST_BITS, bits))
    n_near, n_far = len(near[0]), len(far[0])
    piece = rows // n_near
    parts = exchange(stacked.reshape(n_near, piece, width), near)
    partial = call(
        sum_and_repeat_body, shape((n_far, piece, width), bf16), (10**5, 10**6), parts
    )
    parts = exchange(partial, far)
    total = call(sum_and_repeat_body, shape((n_near, piece, width), bf16), (10**5, 10**6), parts)
    return exchange(total, near).reshape(rows, width)


def per_device(features, w_self, w_neigh, neighbors, degree, boundary, upstream):
    devices = lax.axis_size("dom")
    levels = devices.bit_length() - 1
    node_dev, width = features.shape
    boundary_rows = boundary[0]
    bnd = boundary_rows.shape[1]
    rows = node_dev + levels * bnd

    def swapped(x, level):
        return lax.ppermute(x, "dom", [(i, i ^ 1 << level) for i in range(devices)])

    sent = call(
        send_body, [shape((bnd, width), bf16)] * levels, (3 * 10**8, 10**6), boundary_rows, features
    )
    received = [swapped(x, level) for level, x in enumerate(sent)]
    degree_row = degree.reshape(1, node_dev)
    counts = call(
        count_body, shape((rows, node_dev), bf16), (10**7, 2 * 10**6), neighbors.T, degree_row
    )
    hidden, stacked, local, *returned = call(
        lambda *refs: layer_body(levels, *refs),
        [
            shape((node_dev, width), bf16),
            shape((2 * width, width), f32),
            shape((node_dev, width), f32),
        ]
        + [shape((bnd, width), bf16)] * levels,
        (10**9, 6 * 10**6),
        counts,
        features,
        degree_row,
        upstream,
        w_self,
        w_neigh,
        *received,
        scratch=[pltpu.VMEM((rows, width), bf16)],
    )
    back = [swapped(x, level) for level, x in enumerate(returned)]
    total = total_over_devices(stacked, devices)
    weight_step = call(normalize_body, shape(total.shape, f32), (10**6, 10**6), total)
    node_grad = call(
        collect_body, shape((node_dev, width), bf16), (3 * 10**8, 10**6), boundary_rows, local, *back
    )
    return (hidden, node_grad, weight_step)


def solution(mesh):
    return jax.shard_map(
        per_device,
        mesh=mesh,
        in_specs=(
            P("dom", None),
            P(),
            P(),
            P("dom", None),
            P("dom"),
            P("dom", None, None),
            P("dom", None),
        ),
        out_specs=(P("dom", None), P("dom", None), P()),
        check_vma=False,
    )
```

```python
import jax
import jax.numpy as jnp
from jax import lax
from jax.experimental import pallas as pl
from jax.experimental.pallas import tpu as pltpu
from jax.sharding import PartitionSpec as P

epsilon = 1e-06
f32 = jnp.float32
bf16 = jnp.bfloat16
FAST_BITS = 5
VMEM_LIMIT = 48 * 1024 * 1024
TRANSPOSED_LHS = (((0,), (0,)), ((), ()))
TRANSPOSED_RHS = (((1,), (1,)), ((), ()))


def dot(a, b, dims=(((1,), (0,)), ((), ()))):
    return lax.dot_general(a, b, dims, preferred_element_type=f32)


def call(body, outs, cost, *args, scratch=()):
    flops, moved = cost
    return pl.pallas_call(
        body,
        out_shape=outs,
        scratch_shapes=scratch,
        compiler_params=pltpu.CompilerParams(vmem_limit_bytes=VMEM_LIMIT),
        cost_estimate=pl.CostEstimate(flops=flops, bytes_accessed=moved, transcendentals=0),
    )(*args)


def shape(dims, dtype):
    return jax.ShapeDtypeStruct(dims, dtype)


def one_hot_columns(rows, node_dev):
    k = rows.shape[1]
    ids = lax.broadcasted_iota(jnp.int32, (node_dev, k), 0)
    return jnp.where(ids == rows, f32(1.0), f32(0.0)).astype(bf16)


def core_index():
    return lax.rem(lax.axis_index("dom"), 2)


def level_of(pair, core):
    return jnp.where(core == 0, pair[0], pair[1])


def send_body(pairs, boundary_ref, features_ref, own_ref, lent_ref):
    node_dev = features_ref.shape[0]
    bnd = boundary_ref.shape[1]
    core = core_index()
    features = features_ref[...]

    def rows_of(level):
        pick = one_hot_columns(boundary_ref[pl.ds(level, 1), :], node_dev)
        return dot(pick, features, TRANSPOSED_LHS).astype(bf16)

    lent_ref[:bnd, :] = rows_of(0)
    for k, pair in enumerate(pairs):
        lent_ref[(k + 1) * bnd : (k + 2) * bnd, :] = rows_of(level_of(pair, 1 - core))
        own_ref[k * bnd : (k + 1) * bnd, :] = rows_of(level_of(pair, core))


def load_body(own_ref, borrowed_ref, *load_refs):
    bnd = load_refs[0].shape[0] // 2
    for k, load_ref in enumerate(load_refs):
        load_ref[:bnd, :] = own_ref[k * bnd : (k + 1) * bnd, :]
        load_ref[bnd:, :] = borrowed_ref[(k + 1) * bnd : (k + 2) * bnd, :]


def unload_body(*refs):
    load_refs, lent_ref = refs[:-1], refs[-1]
    bnd = load_refs[0].shape[0] // 2
    for k, load_ref in enumerate(load_refs):
        lent_ref[k * bnd : (k + 1) * bnd, :] = load_ref[bnd:, :]


def count_body(neighbors_ref, degree_ref, counts_ref):
    slots, node_dev = neighbors_ref.shape
    degree = degree_ref[...]
    live = [
        jnp.where(degree > slot, neighbors_ref[slot : slot + 1, :], -1) for slot in range(slots)
    ]
    tile, step = 128, 16
    ids = lax.broadcasted_iota(jnp.int32, (step, node_dev), 0)

    def block(at, carry):
        start = pl.multiple_of(at * tile, tile)
        near = [
            jnp.broadcast_to(row - start, (step, node_dev)).astype(f32).astype(bf16) for row in live
        ]
        for part in range(tile // step):
            here = (ids + part * step).astype(f32).astype(bf16)
            total = jnp.zeros((step, node_dev), bf16)
            for row in near:
                total = total + jnp.where(here == row, bf16(1.0), bf16(0.0))
            counts_ref[pl.ds(start + part * step, step), :] = total
        return carry

    lax.fori_loop(0, counts_ref.shape[0] // tile, block, 0)


def layer_body(pairs, *refs):
    counts_ref, features_ref, degree_ref, upstream_ref, w_self_ref, w_neigh_ref = refs[:6]
    borrowed_ref, kept_ref = refs[6:8]
    loads = refs[8 : 8 + len(pairs)]
    hidden_ref, stacked_ref, local_ref, own_ref, lent_ref, extended_ref = refs[8 + len(pairs) :]
    node_dev, width = features_ref.shape
    bnd = loads[0].shape[0] // 2
    core = core_index()

    def level_rows(level):
        return pl.ds(pl.multiple_of(node_dev + level * bnd, bnd), bnd)

    extended_ref[:node_dev, :] = features_ref[...]
    extended_ref[node_dev : node_dev + bnd, :] = borrowed_ref[:bnd, :]
    for k, pair in enumerate(pairs):
        extended_ref[level_rows(level_of(pair, core)), :] = loads[k][:bnd, :]
        extended_ref[level_rows(level_of(pair, 1 - core)), :] = kept_ref[k * bnd : (k + 1) * bnd, :]
    degree = degree_ref[...].astype(f32)
    degree = jnp.transpose(jnp.broadcast_to(degree, (128, node_dev)))
    degree = jnp.concatenate([degree] * (width // 128), axis=1)
    agg = (dot(counts_ref[...], extended_ref[...], TRANSPOSED_LHS) / degree).astype(bf16)
    features = features_ref[...]
    pre_sum = dot(features, w_self_ref[...]) + dot(agg, w_neigh_ref[...])
    sigmoid_pre = jax.nn.sigmoid(pre_sum)
    hidden_ref[...] = (pre_sum * sigmoid_pre).astype(bf16)
    pre_grad = (
        upstream_ref[...].astype(f32) * sigmoid_pre * (1.0 + pre_sum * (1.0 - sigmoid_pre))
    ).astype(bf16)
    stacked_ref[:width, :] = dot(features, pre_grad, TRANSPOSED_LHS)
    stacked_ref[width:, :] = dot(agg, pre_grad, TRANSPOSED_LHS)
    share = (dot(pre_grad, w_neigh_ref[...], TRANSPOSED_RHS) / degree).astype(bf16)
    lent_ref[:bnd, :] = dot(counts_ref[node_dev : node_dev + bnd, :], share).astype(bf16)
    for k, pair in enumerate(pairs):
        lent_ref[(k + 1) * bnd : (k + 2) * bnd, :] = dot(
            counts_ref[level_rows(level_of(pair, 1 - core)), :], share
        ).astype(bf16)
        own_ref[k * bnd : (k + 1) * bnd, :] = dot(
            counts_ref[level_rows(level_of(pair, core)), :], share
        ).astype(bf16)
    local_ref[...] = dot(pre_grad, w_self_ref[...], TRANSPOSED_RHS) + dot(
        counts_ref[:node_dev, :], share
    )


def collect_body(pairs, boundary_ref, local_ref, borrowed_ref, kept_ref, *refs):
    loads, node_grad_ref = refs[:-1], refs[-1]
    node_dev = local_ref.shape[0]
    bnd = boundary_ref.shape[1]
    core = core_index()

    def added(level, rows):
        return dot(one_hot_columns(boundary_ref[pl.ds(level, 1), :], node_dev), rows)

    total = local_ref[...] + added(0, borrowed_ref[:bnd, :])
    for k, pair in enumerate(pairs):
        total = total + added(level_of(pair, core), loads[k][:bnd, :])
        total = total + added(level_of(pair, 1 - core), kept_ref[k * bnd : (k + 1) * bnd, :])
    node_grad_ref[...] = total.astype(bf16)


def sum_and_repeat_body(parts_ref, out_ref):
    total = parts_ref[0].astype(f32)
    for part in range(1, parts_ref.shape[0]):
        total = total + parts_ref[part].astype(f32)
    out_ref[...] = jnp.broadcast_to(total.astype(out_ref.dtype)[None], out_ref.shape)


def normalize_body(total_ref, out_ref):
    total = total_ref[...].astype(f32)
    mean = jnp.sum(total * total) / total.size
    out_ref[...] = total * lax.rsqrt(jnp.full((1, total.shape[1]), mean + epsilon, f32))


def bit_groups(devices, bits):
    mask = sum(1 << b for b in bits)
    groups = {}
    for i in range(devices):
        groups.setdefault(i & ~mask, []).append(i)
    return list(groups.values())


def exchange(x, groups):
    return lax.all_to_all(x, "dom", 0, 0, axis_index_groups=groups, tiled=True)


def total_over_devices(stacked, devices):
    bits = devices.bit_length() - 1
    rows, width = stacked.shape
    near = bit_groups(devices, range(FAST_BITS))
    far = bit_groups(devices, range(FAST_BITS, bits))
    n_near, n_far = len(near[0]), len(far[0])
    piece = rows // n_near
    parts = exchange(stacked.reshape(n_near, piece, width), near)
    partial = call(
        sum_and_repeat_body, shape((n_far, piece, width), bf16), (10**5, 10**6), parts
    )
    parts = exchange(partial, far)
    total = call(sum_and_repeat_body, shape((n_near, piece, width), bf16), (10**5, 10**6), parts)
    return exchange(total, near).reshape(rows, width)


def level_pairs(levels):
    pairs = []
    for top in range(levels - 1, 1, -2):
        pairs.append((top, top - 1) if not pairs else (top - 1, top))
    return pairs


def per_device(features, w_self, w_neigh, neighbors, degree, boundary, upstream):
    devices = lax.axis_size("dom")
    levels = devices.bit_length() - 1
    pairs = level_pairs(levels)
    node_dev, width = features.shape
    boundary_rows = boundary[0]
    bnd = boundary_rows.shape[1]
    rows = node_dev + levels * bnd
    own_shape = shape((len(pairs) * bnd, width), bf16)
    lent_shape = shape(((len(pairs) + 1) * bnd, width), bf16)
    load_shape = shape((2 * bnd, width), bf16)

    def other_core(x):
        return lax.ppermute(x, "dom", [(i, i ^ 1) for i in range(devices)])

    def carried(own, lent):
        borrowed = other_core(lent)
        loads = call(load_body, [load_shape] * len(pairs), (10**5, 10**6), own, borrowed)
        loads = [
            lax.ppermute(x, "dom", [(i, i ^ 1 << pair[i % 2]) for i in range(devices)])
            for x, pair in zip(loads, pairs)
        ]
        kept = other_core(call(unload_body, own_shape, (10**5, 10**6), *loads))
        return borrowed, kept, *loads

    own, lent = call(
        lambda *refs: send_body(pairs, *refs),
        [own_shape, lent_shape],
        (3 * 10**8, 10**6),
        boundary_rows,
        features,
    )
    received = carried(own, lent)
    degree_row = degree.reshape(1, node_dev)
    counts = call(
        count_body, shape((rows, node_dev), bf16), (10**7, 2 * 10**6), neighbors.T, degree_row
    )
    hidden, stacked, local, own, lent = call(
        lambda *refs: layer_body(pairs, *refs),
        [
            shape((node_dev, width), bf16),
            shape((2 * width, width), f32),
            shape((node_dev, width), f32),
            own_shape,
            lent_shape,
        ],
        (10**9, 6 * 10**6),
        counts,
        features,
        degree_row,
        upstream,
        w_self,
        w_neigh,
        *received,
        scratch=[pltpu.VMEM((rows, width), bf16)],
    )
    back = carried(own, lent)
    total = total_over_devices(stacked, devices)
    weight_step = call(normalize_body, shape(total.shape, f32), (10**6, 10**6), total)
    node_grad = call(
        lambda *refs: collect_body(pairs, *refs),
        shape((node_dev, width), bf16),
        (3 * 10**8, 10**6),
        boundary_rows,
        local,
        *back,
    )
    return (hidden, node_grad, weight_step)


def solution(mesh):
    return jax.shard_map(
        per_device,
        mesh=mesh,
        in_specs=(
            P("dom", None),
            P(),
            P(),
            P("dom", None),
            P("dom"),
            P("dom", None, None),
            P("dom", None),
        ),
        out_specs=(P("dom", None), P("dom", None), P()),
        check_vma=False,
    )
```

```python
import jax
import jax.numpy as jnp
from jax import lax
from jax.experimental import pallas as pl
from jax.experimental.pallas import tpu as pltpu
from jax.sharding import PartitionSpec as P

epsilon = 1e-06
f32 = jnp.float32
bf16 = jnp.bfloat16
FAST_BITS = 5
VMEM_LIMIT = 16 * 1024 * 1024
TRANSPOSED_LHS = (((0,), (0,)), ((), ()))
TRANSPOSED_RHS = (((1,), (1,)), ((), ()))


def dot(a, b, dims=(((1,), (0,)), ((), ()))):
    return lax.dot_general(a, b, dims, preferred_element_type=f32)


def call(body, outs, cost, *args, after=(), scratch=()):
    flops, moved = cost
    reads, waits = len(args), len(after)
    return pl.pallas_call(
        lambda *refs: body(*refs[:reads], *refs[reads + waits :]),
        out_shape=outs,
        in_specs=[pl.BlockSpec(memory_space=pltpu.VMEM)] * reads
        + [pl.BlockSpec(memory_space=pl.ANY)] * waits,
        scratch_shapes=scratch,
        compiler_params=pltpu.CompilerParams(vmem_limit_bytes=VMEM_LIMIT),
        cost_estimate=pl.CostEstimate(flops=flops, bytes_accessed=moved, transcendentals=0),
    )(*args, *after)


def shape(dims, dtype):
    return jax.ShapeDtypeStruct(dims, dtype)


def one_hot_columns(rows, node_dev):
    k = rows.shape[1]
    ids = lax.broadcasted_iota(jnp.int32, (node_dev, k), 0)
    return jnp.where(ids == rows, f32(1.0), f32(0.0)).astype(bf16)


def core_index():
    return lax.rem(lax.axis_index("dom"), 2)


def level_of(pair, core):
    return jnp.where(core == 0, pair[0], pair[1])


def send_body(pairs, boundary_ref, features_ref, own_ref, lent_ref):
    node_dev = features_ref.shape[0]
    bnd = boundary_ref.shape[2]
    core = core_index()
    features = features_ref[...]

    def rows_of(level):
        pick = one_hot_columns(boundary_ref[level], node_dev)
        return dot(pick, features, TRANSPOSED_LHS).astype(bf16)

    lent_ref[:bnd, :] = rows_of(0)
    for k, pair in enumerate(pairs):
        lent_ref[(k + 1) * bnd : (k + 2) * bnd, :] = rows_of(level_of(pair, 1 - core))
        own_ref[k * bnd : (k + 1) * bnd, :] = rows_of(level_of(pair, core))


def load_body(first, skip, own_ref, borrowed_ref, *load_refs):
    bnd = load_refs[0].shape[0] // 2
    for k, load_ref in enumerate(load_refs):
        load_ref[:bnd, :] = own_ref[(k + first) * bnd : (k + first + 1) * bnd, :]
        load_ref[bnd:, :] = borrowed_ref[(k + skip) * bnd : (k + skip + 1) * bnd, :]


def unload_body(*refs):
    load_refs, lent_ref = refs[:-1], refs[-1]
    bnd = load_refs[0].shape[0] // 2
    for k, load_ref in enumerate(load_refs):
        lent_ref[k * bnd : (k + 1) * bnd, :] = load_ref[bnd:, :]


def count_body(neighbors_ref, degree_ref, counts_ref):
    slots, node_dev = neighbors_ref.shape
    degree = degree_ref[...]
    live = [
        jnp.where(degree > slot, neighbors_ref[slot : slot + 1, :], -1) for slot in range(slots)
    ]
    tile, step = 128, 16
    ids = lax.broadcasted_iota(jnp.int32, (step, node_dev), 0)

    def block(at, carry):
        start = pl.multiple_of(at * tile, tile)
        near = [
            jnp.broadcast_to(row - start, (step, node_dev)).astype(f32).astype(bf16) for row in live
        ]
        for part in range(tile // step):
            here = (ids + part * step).astype(f32).astype(bf16)
            total = jnp.zeros((step, node_dev), bf16)
            for row in near:
                total = total + jnp.where(here == row, bf16(1.0), bf16(0.0))
            counts_ref[pl.ds(start + part * step, step), :] = total
        return carry

    lax.fori_loop(0, counts_ref.shape[0] // tile, block, 0)


def gather_early_body(pairs, counts_ref, features_ref, w_self_ref, borrowed_ref, *refs):
    loads, summed_ref, own_part_ref = refs[:-2], refs[-2], refs[-1]
    node_dev = features_ref.shape[0]
    bnd = borrowed_ref.shape[0] // (len(pairs) + 1)
    core = core_index()
    features = features_ref[...]
    own_part_ref[...] = dot(features, w_self_ref[...])
    summed = dot(counts_ref[:node_dev, :], features, TRANSPOSED_LHS)
    summed = summed + dot(
        counts_ref[node_dev : node_dev + bnd, :], borrowed_ref[:bnd, :], TRANSPOSED_LHS
    )
    for k, pair in enumerate(pairs):
        rows = level_rows(node_dev, bnd, level_of(pair, core))
        summed = summed + dot(counts_ref[rows, :], loads[k][:bnd, :], TRANSPOSED_LHS)
    summed_ref[...] = summed


def level_rows(node_dev, bnd, level):
    return pl.ds(pl.multiple_of(node_dev + level * bnd, bnd), bnd)


def layer_body(
    pairs,
    counts_ref,
    summed_ref,
    own_part_ref,
    kept_ref,
    features_ref,
    degree_ref,
    upstream_ref,
    w_neigh_ref,
    hidden_ref,
    stacked_ref,
    pre_grad_ref,
    share_ref,
):
    node_dev, width = features_ref.shape
    bnd = kept_ref.shape[0] // len(pairs)
    core = core_index()
    degree = degree_ref[...].astype(f32)
    degree = jnp.transpose(jnp.broadcast_to(degree, (128, node_dev)))
    degree = jnp.concatenate([degree] * (width // 128), axis=1)
    summed = summed_ref[...]
    for k, pair in enumerate(pairs):
        rows = level_rows(node_dev, bnd, level_of(pair, 1 - core))
        kept = kept_ref[k * bnd : (k + 1) * bnd, :]
        summed = summed + dot(counts_ref[rows, :], kept, TRANSPOSED_LHS)
    agg = (summed / degree).astype(bf16)
    pre_sum = own_part_ref[...] + dot(agg, w_neigh_ref[...])
    sigmoid_pre = jax.nn.sigmoid(pre_sum)
    hidden_ref[...] = (pre_sum * sigmoid_pre).astype(bf16)
    pre_grad = (
        upstream_ref[...].astype(f32) * sigmoid_pre * (1.0 + pre_sum * (1.0 - sigmoid_pre))
    ).astype(bf16)
    stacked_ref[:width, :] = dot(features_ref[...], pre_grad, TRANSPOSED_LHS).astype(bf16)
    stacked_ref[width:, :] = dot(agg, pre_grad, TRANSPOSED_LHS).astype(bf16)
    share = (dot(pre_grad, w_neigh_ref[...], TRANSPOSED_RHS) / degree).astype(bf16)
    pre_grad_ref[...] = pre_grad
    share_ref[...] = share


def spread_body(
    pairs, counts_ref, pre_grad_ref, share_ref, w_self_ref, local_ref, own_ref, lent_a_ref, lent_b_ref
):
    node_dev = pre_grad_ref.shape[0]
    bnd = own_ref.shape[0] // len(pairs)
    core = core_index()
    pre_grad, share = pre_grad_ref[...], share_ref[...]
    split = lent_a_ref.shape[0] // bnd
    for k, pair in enumerate(pairs):
        rows = level_rows(node_dev, bnd, level_of(pair, 1 - core))
        lent_ref, at = (lent_a_ref, k) if k < split else (lent_b_ref, k - split)
        lent_ref[at * bnd : (at + 1) * bnd, :] = dot(counts_ref[rows, :], share).astype(bf16)
        rows = level_rows(node_dev, bnd, level_of(pair, core))
        own_ref[k * bnd : (k + 1) * bnd, :] = dot(counts_ref[rows, :], share).astype(bf16)
    lent_b_ref[(len(pairs) - split) * bnd :, :] = dot(
        counts_ref[node_dev : node_dev + bnd, :], share
    ).astype(bf16)
    local_ref[...] = dot(pre_grad, w_self_ref[...], TRANSPOSED_RHS) + dot(
        counts_ref[:node_dev, :], share
    )


def collect_early_body(pairs, boundary_ref, local_ref, borrowed_ref, *refs):
    loads, sum_ref = refs[:-1], refs[-1]
    node_dev = local_ref.shape[0]
    bnd = boundary_ref.shape[2]
    core = core_index()
    pick = one_hot_columns(boundary_ref[0], node_dev)
    total = local_ref[...] + dot(pick, borrowed_ref[borrowed_ref.shape[0] - bnd :, :])
    for k, pair in enumerate(pairs):
        pick = one_hot_columns(boundary_ref[level_of(pair, core)], node_dev)
        total = total + dot(pick, loads[k][:bnd, :])
    sum_ref[...] = total


def collect_body(pairs, boundary_ref, sum_ref, kept_ref, node_grad_ref):
    node_dev = sum_ref.shape[0]
    bnd = boundary_ref.shape[2]
    core = core_index()
    total = sum_ref[...]
    for k, pair in enumerate(pairs):
        pick = one_hot_columns(boundary_ref[level_of(pair, 1 - core)], node_dev)
        total = total + dot(pick, kept_ref[k * bnd : (k + 1) * bnd, :])
    node_grad_ref[...] = total.astype(bf16)


def normalize_body(total_ref, out_ref):
    total = total_ref[...].astype(f32)
    mean = jnp.sum(total * total) / total.size
    out_ref[...] = total * lax.rsqrt(jnp.full((1, total.shape[1]), mean + epsilon, f32))


def sum_and_repeat_body(parts_ref, out_ref):
    total = parts_ref[0].astype(f32)
    for part in range(1, parts_ref.shape[0]):
        total = total + parts_ref[part].astype(f32)
    out_ref[...] = jnp.broadcast_to(total.astype(out_ref.dtype)[None], out_ref.shape)


def bit_groups(devices, bits):
    mask = sum(1 << b for b in bits)
    groups = {}
    for i in range(devices):
        groups.setdefault(i & ~mask, []).append(i)
    return list(groups.values())


def exchange(x, groups):
    return lax.all_to_all(x, "dom", 0, 0, axis_index_groups=groups, tiled=True)


def level_pairs(levels):
    pairs = []
    for top in range(levels - 1, 1, -2):
        pairs.append((top, top - 1) if not pairs else (top - 1, top))
    return pairs


def per_device(features, w_self, w_neigh, neighbors, degree, boundary, upstream):
    devices = lax.axis_size("dom")
    levels = devices.bit_length() - 1
    pairs = level_pairs(levels)
    node_dev, width = features.shape
    boundary_rows = boundary.transpose(1, 0, 2)
    bnd = boundary_rows.shape[2]
    rows = node_dev + levels * bnd
    block = (node_dev, width)
    own_shape = shape((len(pairs) * bnd, width), bf16)
    lent_shape = shape(((len(pairs) + 1) * bnd, width), bf16)
    load_shape = shape((2 * bnd, width), bf16)
    near = bit_groups(devices, range(FAST_BITS))
    far = bit_groups(devices, range(FAST_BITS, levels))
    piece = 2 * width // len(near[0])
    small = (10**8, 10**6)

    def other_core(x):
        return lax.ppermute(x, "dom", [(i, i ^ 1) for i in range(devices)])

    def across(loads, taken):
        return [
            lax.ppermute(x, "dom", [(i, i ^ 1 << pair[i % 2]) for i in range(devices)])
            for x, pair in zip(loads, taken)
        ]

    def with_pairs(body):
        return lambda *refs: body(pairs, *refs)

    def loaded(own, borrowed, first, last, skip=0):
        return call(
            lambda *refs: load_body(first, skip, *refs),
            [load_shape] * (last - first),
            small,
            own,
            borrowed,
        )

    own, lent = call(
        with_pairs(send_body), [own_shape, lent_shape], (10**9, 10**6), boundary_rows, features
    )
    borrowed = other_core(lent)
    loads = loaded(own, borrowed, 0, len(pairs), skip=1)
    degree_row = degree.reshape(1, node_dev)
    counts = call(
        count_body,
        shape((rows, node_dev), bf16),
        (2 * 10**9, 2 * 10**6),
        neighbors.T,
        degree_row,
        after=(loads[-1],),
    )
    loads = across(loads, pairs)
    kept = other_core(call(unload_body, own_shape, small, *loads, after=(counts,)))
    summed, own_part = call(
        with_pairs(gather_early_body),
        [shape(block, f32)] * 2,
        (10**9, 3 * 10**6),
        counts,
        features,
        w_self,
        borrowed,
        *loads,
    )
    hidden, stacked, pre_grad, share = call(
        with_pairs(layer_body),
        [
            shape(block, bf16),
            shape((2 * width, width), bf16),
            shape(block, bf16),
            shape(block, bf16),
        ],
        (2 * 10**9, 5 * 10**6),
        counts,
        summed,
        own_part,
        kept,
        features,
        degree_row,
        upstream,
        w_neigh,
    )

    parts = exchange(stacked.reshape(len(near[0]), piece, width), near)
    split = len(pairs) // 2
    local, own, lent_a, lent_b = call(
        with_pairs(spread_body),
        [
            shape(block, f32),
            own_shape,
            shape((split * bnd, width), bf16),
            shape(((len(pairs) - split + 1) * bnd, width), bf16),
        ],
        small,
        counts,
        pre_grad,
        share,
        w_self,
    )
    borrowed_a, borrowed_b = other_core(lent_a), other_core(lent_b)
    partial = call(
        sum_and_repeat_body,
        shape((len(far[0]), piece, width), bf16),
        small,
        parts,
        after=(borrowed_a, borrowed_b),
    )
    parts = exchange(partial, far)
    loads = loaded(own, borrowed_a, 0, split) + loaded(own, borrowed_b, split, len(pairs))
    loads = across(loads, pairs)
    total = call(sum_and_repeat_body, shape((len(near[0]), piece, width), bf16), small, parts)
    gathered = exchange(total, near).reshape(2 * width, width)
    kept = other_core(call(unload_body, own_shape, small, *loads, after=(total,)))
    early = call(
        with_pairs(collect_early_body),
        shape(block, f32),
        (10**9, 10**6),
        boundary_rows,
        local,
        borrowed_b,
        *loads,
    )
    node_grad = call(
        with_pairs(collect_body), shape(block, bf16), (10**9, 10**6), boundary_rows, early, kept
    )
    weight_step = call(normalize_body, shape(gathered.shape, f32), small, gathered)
    return (hidden, node_grad, weight_step)


def solution(mesh):
    return jax.shard_map(
        per_device,
        mesh=mesh,
        in_specs=(
            P("dom", None),
            P(),
            P(),
            P("dom", None),
            P("dom"),
            P("dom", None, None),
            P("dom", None),
        ),
        out_specs=(P("dom", None), P("dom", None), P()),
        check_vma=False,
    )
```

```python
import jax
import jax.numpy as jnp
from jax import lax
from jax.experimental import pallas as pl
from jax.experimental.pallas import tpu as pltpu
from jax.sharding import PartitionSpec as P

epsilon = 1e-06
f32 = jnp.float32
bf16 = jnp.bfloat16
FAST_BITS = 5
VMEM_LIMIT = 16 * 1024 * 1024
TRANSPOSED_LHS = (((0,), (0,)), ((), ()))
TRANSPOSED_RHS = (((1,), (1,)), ((), ()))


def dot(a, b, dims=(((1,), (0,)), ((), ()))):
    return lax.dot_general(a, b, dims, preferred_element_type=f32)


def call(body, outs, cost, *args, after=(), scratch=()):
    flops, moved = cost
    reads, waits = len(args), len(after)
    return pl.pallas_call(
        lambda *refs: body(*refs[:reads], *refs[reads + waits :]),
        out_shape=outs,
        in_specs=[pl.BlockSpec(memory_space=pltpu.VMEM)] * reads
        + [pl.BlockSpec(memory_space=pl.ANY)] * waits,
        scratch_shapes=scratch,
        compiler_params=pltpu.CompilerParams(vmem_limit_bytes=VMEM_LIMIT),
        cost_estimate=pl.CostEstimate(flops=flops, bytes_accessed=moved, transcendentals=0),
    )(*args, *after)


def shape(dims, dtype):
    return jax.ShapeDtypeStruct(dims, dtype)


def one_hot_columns(rows, node_dev):
    k = rows.shape[1]
    ids = lax.broadcasted_iota(jnp.int32, (node_dev, k), 0)
    return jnp.where(ids == rows, f32(1.0), f32(0.0)).astype(bf16)


def core_index():
    return lax.rem(lax.axis_index("dom"), 2)


def level_of(pair, core):
    return jnp.where(core == 0, pair[0], pair[1])


def send_body(pairs, boundary_ref, features_ref, own_ref, lent_ref):
    node_dev = features_ref.shape[0]
    bnd = boundary_ref.shape[2]
    core = core_index()
    features = features_ref[...]

    def rows_of(level):
        pick = one_hot_columns(boundary_ref[level], node_dev)
        return dot(pick, features, TRANSPOSED_LHS).astype(bf16)

    lent_ref[:bnd, :] = rows_of(0)
    for k, pair in enumerate(pairs):
        lent_ref[(k + 1) * bnd : (k + 2) * bnd, :] = rows_of(level_of(pair, 1 - core))
        own_ref[k * bnd : (k + 1) * bnd, :] = rows_of(level_of(pair, core))


def load_body(first, skip, own_ref, borrowed_ref, *load_refs):
    bnd = load_refs[0].shape[0] // 2
    for k, load_ref in enumerate(load_refs):
        load_ref[:bnd, :] = own_ref[(k + first) * bnd : (k + first + 1) * bnd, :]
        load_ref[bnd:, :] = borrowed_ref[(k + skip) * bnd : (k + skip + 1) * bnd, :]


def unload_body(*refs):
    load_refs, lent_ref = refs[:-1], refs[-1]
    bnd = load_refs[0].shape[0] // 2
    for k, load_ref in enumerate(load_refs):
        lent_ref[k * bnd : (k + 1) * bnd, :] = load_ref[bnd:, :]


def count_body(neighbors_ref, degree_ref, counts_ref):
    slots, node_dev = neighbors_ref.shape
    degree = degree_ref[...]
    live = [
        jnp.where(degree > slot, neighbors_ref[slot : slot + 1, :], -1) for slot in range(slots)
    ]
    tile, step = 128, 16
    ids = lax.broadcasted_iota(jnp.int32, (step, node_dev), 0)

    def block(at, carry):
        start = pl.multiple_of(at * tile, tile)
        near = [
            jnp.broadcast_to(row - start, (step, node_dev)).astype(f32).astype(bf16) for row in live
        ]
        for part in range(tile // step):
            here = (ids + part * step).astype(f32).astype(bf16)
            total = jnp.zeros((step, node_dev), bf16)
            for row in near:
                total = total + jnp.where(here == row, bf16(1.0), bf16(0.0))
            counts_ref[pl.ds(start + part * step, step), :] = total
        return carry

    lax.fori_loop(0, counts_ref.shape[0] // tile, block, 0)


def gather_early_body(pairs, counts_ref, features_ref, w_self_ref, borrowed_ref, *refs):
    loads, summed_ref, own_part_ref = refs[:-2], refs[-2], refs[-1]
    node_dev = features_ref.shape[0]
    bnd = borrowed_ref.shape[0] // (len(pairs) + 1)
    core = core_index()
    features = features_ref[...]
    own_part_ref[...] = dot(features, w_self_ref[...])
    summed = dot(counts_ref[:node_dev, :], features, TRANSPOSED_LHS)
    summed = summed + dot(
        counts_ref[node_dev : node_dev + bnd, :], borrowed_ref[:bnd, :], TRANSPOSED_LHS
    )
    for k, pair in enumerate(pairs):
        rows = level_rows(node_dev, bnd, level_of(pair, core))
        summed = summed + dot(counts_ref[rows, :], loads[k][:bnd, :], TRANSPOSED_LHS)
    summed_ref[...] = summed


def level_rows(node_dev, bnd, level):
    return pl.ds(pl.multiple_of(node_dev + level * bnd, bnd), bnd)


def layer_body(
    pairs,
    counts_ref,
    summed_ref,
    own_part_ref,
    kept_ref,
    features_ref,
    degree_ref,
    upstream_ref,
    w_neigh_ref,
    hidden_ref,
    stacked_ref,
    pre_grad_ref,
    share_ref,
):
    node_dev, width = features_ref.shape
    bnd = kept_ref.shape[0] // len(pairs)
    core = core_index()
    degree = degree_ref[...].astype(f32)
    degree = jnp.transpose(jnp.broadcast_to(degree, (128, node_dev)))
    degree = jnp.concatenate([degree] * (width // 128), axis=1)
    summed = summed_ref[...]
    for k, pair in enumerate(pairs):
        rows = level_rows(node_dev, bnd, level_of(pair, 1 - core))
        kept = kept_ref[k * bnd : (k + 1) * bnd, :]
        summed = summed + dot(counts_ref[rows, :], kept, TRANSPOSED_LHS)
    agg = (summed / degree).astype(bf16)
    pre_sum = own_part_ref[...] + dot(agg, w_neigh_ref[...])
    sigmoid_pre = jax.nn.sigmoid(pre_sum)
    hidden_ref[...] = (pre_sum * sigmoid_pre).astype(bf16)
    pre_grad = (
        upstream_ref[...].astype(f32) * sigmoid_pre * (1.0 + pre_sum * (1.0 - sigmoid_pre))
    ).astype(bf16)
    stacked_ref[:width, :] = dot(features_ref[...], pre_grad, TRANSPOSED_LHS).astype(bf16)
    stacked_ref[width:, :] = dot(agg, pre_grad, TRANSPOSED_LHS).astype(bf16)
    share = (dot(pre_grad, w_neigh_ref[...], TRANSPOSED_RHS) / degree).astype(bf16)
    pre_grad_ref[...] = pre_grad
    share_ref[...] = share


def spread_body(
    pairs, counts_ref, pre_grad_ref, share_ref, w_self_ref, local_ref, own_ref, lent_a_ref, lent_b_ref
):
    node_dev = pre_grad_ref.shape[0]
    bnd = own_ref.shape[0] // len(pairs)
    core = core_index()
    pre_grad, share = pre_grad_ref[...], share_ref[...]
    split = lent_a_ref.shape[0] // bnd
    for k, pair in enumerate(pairs):
        rows = level_rows(node_dev, bnd, level_of(pair, 1 - core))
        lent_ref, at = (lent_a_ref, k) if k < split else (lent_b_ref, k - split)
        lent_ref[at * bnd : (at + 1) * bnd, :] = dot(counts_ref[rows, :], share).astype(bf16)
        rows = level_rows(node_dev, bnd, level_of(pair, core))
        own_ref[k * bnd : (k + 1) * bnd, :] = dot(counts_ref[rows, :], share).astype(bf16)
    lent_b_ref[(len(pairs) - split) * bnd :, :] = dot(
        counts_ref[node_dev : node_dev + bnd, :], share
    ).astype(bf16)
    local_ref[...] = dot(pre_grad, w_self_ref[...], TRANSPOSED_RHS) + dot(
        counts_ref[:node_dev, :], share
    )


def collect_early_body(pairs, boundary_ref, local_ref, borrowed_ref, *refs):
    loads, sum_ref = refs[:-1], refs[-1]
    node_dev = local_ref.shape[0]
    bnd = boundary_ref.shape[2]
    core = core_index()
    pick = one_hot_columns(boundary_ref[0], node_dev)
    total = local_ref[...] + dot(pick, borrowed_ref[borrowed_ref.shape[0] - bnd :, :])
    for k, pair in enumerate(pairs):
        pick = one_hot_columns(boundary_ref[level_of(pair, core)], node_dev)
        total = total + dot(pick, loads[k][:bnd, :])
    sum_ref[...] = total


def collect_body(pairs, boundary_ref, sum_ref, kept_ref, node_grad_ref):
    node_dev = sum_ref.shape[0]
    bnd = boundary_ref.shape[2]
    core = core_index()
    total = sum_ref[...]
    for k, pair in enumerate(pairs):
        pick = one_hot_columns(boundary_ref[level_of(pair, 1 - core)], node_dev)
        total = total + dot(pick, kept_ref[k * bnd : (k + 1) * bnd, :])
    node_grad_ref[...] = total.astype(bf16)


def normalize_body(total_ref, out_ref):
    total = total_ref[...].astype(f32)
    mean = jnp.sum(total * total) / total.size
    out_ref[...] = total * lax.rsqrt(jnp.full((1, total.shape[1]), mean + epsilon, f32))


def sum_and_repeat_body(parts_ref, out_ref):
    total = parts_ref[0].astype(f32)
    for part in range(1, parts_ref.shape[0]):
        total = total + parts_ref[part].astype(f32)
    out_ref[...] = jnp.broadcast_to(total.astype(out_ref.dtype)[None], out_ref.shape)


def bit_groups(devices, bits):
    mask = sum(1 << b for b in bits)
    groups = {}
    for i in range(devices):
        groups.setdefault(i & ~mask, []).append(i)
    return list(groups.values())


def exchange(x, groups):
    return lax.all_to_all(x, "dom", 0, 0, axis_index_groups=groups, tiled=True)


def level_pairs(levels):
    pairs = []
    for top in range(levels - 1, 1, -2):
        pairs.append((top, top - 1) if not pairs else (top - 1, top))
    return pairs


def per_device(features, w_self, w_neigh, neighbors, degree, boundary, upstream):
    devices = lax.axis_size("dom")
    levels = devices.bit_length() - 1
    pairs = level_pairs(levels)
    node_dev, width = features.shape
    boundary_rows = boundary.transpose(1, 0, 2)
    bnd = boundary_rows.shape[2]
    rows = node_dev + levels * bnd
    block = (node_dev, width)
    own_shape = shape((len(pairs) * bnd, width), bf16)
    lent_shape = shape(((len(pairs) + 1) * bnd, width), bf16)
    load_shape = shape((2 * bnd, width), bf16)
    near = bit_groups(devices, range(FAST_BITS))
    far = bit_groups(devices, range(FAST_BITS, levels))
    far = [group[len(group) // 2 :] + group[: len(group) // 2] for group in far]
    piece = 2 * width // len(near[0])
    small = (10**8, 10**6)

    def other_core(x):
        return lax.ppermute(x, "dom", [(i, i ^ 1) for i in range(devices)])

    def across(loads, taken):
        return [
            lax.ppermute(x, "dom", [(i, i ^ 1 << pair[i % 2]) for i in range(devices)])
            for x, pair in zip(loads, taken)
        ]

    def with_pairs(body):
        return lambda *refs: body(pairs, *refs)

    def loaded(own, borrowed, first, last, skip=0):
        return call(
            lambda *refs: load_body(first, skip, *refs),
            [load_shape] * (last - first),
            small,
            own,
            borrowed,
        )

    own, lent = call(
        with_pairs(send_body), [own_shape, lent_shape], (10**9, 10**6), boundary_rows, features
    )
    borrowed = other_core(lent)
    loads = loaded(own, borrowed, 0, len(pairs), skip=1)
    degree_row = degree.reshape(1, node_dev)
    counts = call(
        count_body,
        shape((rows, node_dev), bf16),
        (2 * 10**9, 2 * 10**6),
        neighbors.T,
        degree_row,
        after=(loads[-1],),
    )
    loads = across(loads, pairs)
    kept = other_core(call(unload_body, own_shape, small, *loads, after=(counts,)))
    summed, own_part = call(
        with_pairs(gather_early_body),
        [shape(block, f32)] * 2,
        (10**9, 3 * 10**6),
        counts,
        features,
        w_self,
        borrowed,
        *loads,
    )
    hidden, stacked, pre_grad, share = call(
        with_pairs(layer_body),
        [
            shape(block, bf16),
            shape((2 * width, width), bf16),
            shape(block, bf16),
            shape(block, bf16),
        ],
        (2 * 10**9, 5 * 10**6),
        counts,
        summed,
        own_part,
        kept,
        features,
        degree_row,
        upstream,
        w_neigh,
    )

    parts = exchange(stacked.reshape(len(near[0]), piece, width), near)
    split = len(pairs) // 2
    local, own, lent_a, lent_b = call(
        with_pairs(spread_body),
        [
            shape(block, f32),
            own_shape,
            shape((split * bnd, width), bf16),
            shape(((len(pairs) - split + 1) * bnd, width), bf16),
        ],
        small,
        counts,
        pre_grad,
        share,
        w_self,
    )
    borrowed_a, borrowed_b = other_core(lent_a), other_core(lent_b)
    partial = call(
        sum_and_repeat_body,
        shape((len(far[0]), piece, width), bf16),
        small,
        parts,
        after=(borrowed_a, borrowed_b),
    )
    parts = exchange(partial, far)
    loads = loaded(own, borrowed_a, 0, split) + loaded(own, borrowed_b, split, len(pairs))
    loads = across(loads, pairs)
    total = call(sum_and_repeat_body, shape((len(near[0]), piece, width), bf16), small, parts)
    gathered = exchange(total, near).reshape(2 * width, width)
    kept = other_core(call(unload_body, own_shape, small, *loads, after=(total,)))
    early = call(
        with_pairs(collect_early_body),
        shape(block, f32),
        (10**9, 10**6),
        boundary_rows,
        local,
        borrowed_b,
        *loads,
    )
    node_grad = call(
        with_pairs(collect_body), shape(block, bf16), (10**9, 10**6), boundary_rows, early, kept
    )
    weight_step = call(normalize_body, shape(gathered.shape, f32), small, gathered)
    return (hidden, node_grad, weight_step)


def solution(mesh):
    return jax.shard_map(
        per_device,
        mesh=mesh,
        in_specs=(
            P("dom", None),
            P(),
            P(),
            P("dom", None),
            P("dom"),
            P("dom", None, None),
            P("dom", None),
        ),
        out_specs=(P("dom", None), P("dom", None), P()),
        check_vma=False,
    )
```

```python
import jax
import jax.numpy as jnp
from jax import lax
from jax.experimental import pallas as pl
from jax.experimental.pallas import tpu as pltpu
from jax.sharding import PartitionSpec as P

epsilon = 1e-06
f32 = jnp.float32
bf16 = jnp.bfloat16
FAST_BITS = 5
NEAR_FIRST = 20
VMEM_LIMIT = 16 * 1024 * 1024
TRANSPOSED_LHS = (((0,), (0,)), ((), ()))
TRANSPOSED_RHS = (((1,), (1,)), ((), ()))


def dot(a, b, dims=(((1,), (0,)), ((), ()))):
    return lax.dot_general(a, b, dims, preferred_element_type=f32)


def call(body, outs, cost, *args, after=(), scratch=()):
    flops, moved = cost
    reads, waits = len(args), len(after)
    return pl.pallas_call(
        lambda *refs: body(*refs[:reads], *refs[reads + waits :]),
        out_shape=outs,
        in_specs=[pl.BlockSpec(memory_space=pltpu.VMEM)] * reads
        + [pl.BlockSpec(memory_space=pl.ANY)] * waits,
        scratch_shapes=scratch,
        compiler_params=pltpu.CompilerParams(vmem_limit_bytes=VMEM_LIMIT),
        cost_estimate=pl.CostEstimate(flops=flops, bytes_accessed=moved, transcendentals=0),
    )(*args, *after)


def shape(dims, dtype):
    return jax.ShapeDtypeStruct(dims, dtype)


def one_hot_columns(rows, node_dev):
    k = rows.shape[1]
    ids = lax.broadcasted_iota(jnp.int32, (node_dev, k), 0)
    return jnp.where(ids == rows, f32(1.0), f32(0.0)).astype(bf16)


def core_index():
    return lax.rem(lax.axis_index("dom"), 2)


def level_of(pair, core):
    return jnp.where(core == 0, pair[0], pair[1])


def send_body(pairs, boundary_ref, features_ref, own_ref, lent_ref):
    node_dev = features_ref.shape[0]
    bnd = boundary_ref.shape[2]
    core = core_index()
    features = features_ref[...]

    def rows_of(level):
        pick = one_hot_columns(boundary_ref[level], node_dev)
        return dot(pick, features, TRANSPOSED_LHS).astype(bf16)

    lent_ref[:bnd, :] = rows_of(0)
    for k, pair in enumerate(pairs):
        lent_ref[(k + 1) * bnd : (k + 2) * bnd, :] = rows_of(level_of(pair, 1 - core))
        own_ref[k * bnd : (k + 1) * bnd, :] = rows_of(level_of(pair, core))


def load_body(first, skip, own_ref, borrowed_ref, *load_refs):
    bnd = load_refs[0].shape[0] // 2
    for k, load_ref in enumerate(load_refs):
        load_ref[:bnd, :] = own_ref[(k + first) * bnd : (k + first + 1) * bnd, :]
        load_ref[bnd:, :] = borrowed_ref[(k + skip) * bnd : (k + skip + 1) * bnd, :]


def unload_body(*refs):
    load_refs, lent_ref = refs[:-1], refs[-1]
    bnd = load_refs[0].shape[0] // 2
    for k, load_ref in enumerate(load_refs):
        lent_ref[k * bnd : (k + 1) * bnd, :] = load_ref[bnd:, :]


def count_body(neighbors_ref, degree_ref, counts_ref):
    slots, node_dev = neighbors_ref.shape
    degree = degree_ref[...]
    live = [
        jnp.where(degree > slot, neighbors_ref[slot : slot + 1, :], -1) for slot in range(slots)
    ]
    tile, step = 128, 16
    ids = lax.broadcasted_iota(jnp.int32, (step, node_dev), 0)

    def block(at, carry):
        start = pl.multiple_of(at * tile, tile)
        near = [
            jnp.broadcast_to(row - start, (step, node_dev)).astype(f32).astype(bf16) for row in live
        ]
        for part in range(tile // step):
            here = (ids + part * step).astype(f32).astype(bf16)
            total = jnp.zeros((step, node_dev), bf16)
            for row in near:
                total = total + jnp.where(here == row, bf16(1.0), bf16(0.0))
            counts_ref[pl.ds(start + part * step, step), :] = total
        return carry

    lax.fori_loop(0, counts_ref.shape[0] // tile, block, 0)


def gather_early_body(pairs, counts_ref, features_ref, w_self_ref, borrowed_ref, *refs):
    loads, summed_ref, own_part_ref = refs[:-2], refs[-2], refs[-1]
    node_dev = features_ref.shape[0]
    bnd = borrowed_ref.shape[0] // (len(pairs) + 1)
    core = core_index()
    features = features_ref[...]
    own_part_ref[...] = dot(features, w_self_ref[...])
    summed = dot(counts_ref[:node_dev, :], features, TRANSPOSED_LHS)
    summed = summed + dot(
        counts_ref[node_dev : node_dev + bnd, :], borrowed_ref[:bnd, :], TRANSPOSED_LHS
    )
    for k, pair in enumerate(pairs):
        rows = level_rows(node_dev, bnd, level_of(pair, core))
        summed = summed + dot(counts_ref[rows, :], loads[k][:bnd, :], TRANSPOSED_LHS)
    summed_ref[...] = summed


def level_rows(node_dev, bnd, level):
    return pl.ds(pl.multiple_of(node_dev + level * bnd, bnd), bnd)


def layer_body(
    pairs,
    counts_ref,
    summed_ref,
    own_part_ref,
    kept_ref,
    features_ref,
    degree_ref,
    upstream_ref,
    w_neigh_ref,
    hidden_ref,
    stacked_ref,
    pre_grad_ref,
    share_ref,
):
    node_dev, width = features_ref.shape
    bnd = kept_ref.shape[0] // len(pairs)
    core = core_index()
    degree = degree_ref[...].astype(f32)
    degree = jnp.transpose(jnp.broadcast_to(degree, (128, node_dev)))
    degree = jnp.concatenate([degree] * (width // 128), axis=1)
    summed = summed_ref[...]
    for k, pair in enumerate(pairs):
        rows = level_rows(node_dev, bnd, level_of(pair, 1 - core))
        kept = kept_ref[k * bnd : (k + 1) * bnd, :]
        summed = summed + dot(counts_ref[rows, :], kept, TRANSPOSED_LHS)
    agg = (summed / degree).astype(bf16)
    pre_sum = own_part_ref[...] + dot(agg, w_neigh_ref[...])
    sigmoid_pre = jax.nn.sigmoid(pre_sum)
    hidden_ref[...] = (pre_sum * sigmoid_pre).astype(bf16)
    pre_grad = (
        upstream_ref[...].astype(f32) * sigmoid_pre * (1.0 + pre_sum * (1.0 - sigmoid_pre))
    ).astype(bf16)
    stacked_ref[:width, :] = dot(features_ref[...], pre_grad, TRANSPOSED_LHS).astype(bf16)
    stacked_ref[width:, :] = dot(agg, pre_grad, TRANSPOSED_LHS).astype(bf16)
    share = (dot(pre_grad, w_neigh_ref[...], TRANSPOSED_RHS) / degree).astype(bf16)
    pre_grad_ref[...] = pre_grad
    share_ref[...] = share


def spread_body(
    pairs, counts_ref, pre_grad_ref, share_ref, w_self_ref, local_ref, own_ref, lent_a_ref, lent_b_ref
):
    node_dev = pre_grad_ref.shape[0]
    bnd = own_ref.shape[0] // len(pairs)
    core = core_index()
    pre_grad, share = pre_grad_ref[...], share_ref[...]
    split = lent_a_ref.shape[0] // bnd
    for k, pair in enumerate(pairs):
        rows = level_rows(node_dev, bnd, level_of(pair, 1 - core))
        lent_ref, at = (lent_a_ref, k) if k < split else (lent_b_ref, k - split)
        lent_ref[at * bnd : (at + 1) * bnd, :] = dot(counts_ref[rows, :], share).astype(bf16)
        rows = level_rows(node_dev, bnd, level_of(pair, core))
        own_ref[k * bnd : (k + 1) * bnd, :] = dot(counts_ref[rows, :], share).astype(bf16)
    lent_b_ref[(len(pairs) - split) * bnd :, :] = dot(
        counts_ref[node_dev : node_dev + bnd, :], share
    ).astype(bf16)
    local_ref[...] = dot(pre_grad, w_self_ref[...], TRANSPOSED_RHS) + dot(
        counts_ref[:node_dev, :], share
    )


def collect_early_body(pairs, boundary_ref, local_ref, borrowed_ref, *refs):
    loads, sum_ref = refs[:-1], refs[-1]
    node_dev = local_ref.shape[0]
    bnd = boundary_ref.shape[2]
    core = core_index()
    pick = one_hot_columns(boundary_ref[0], node_dev)
    total = local_ref[...] + dot(pick, borrowed_ref[borrowed_ref.shape[0] - bnd :, :])
    for k, pair in enumerate(pairs):
        pick = one_hot_columns(boundary_ref[level_of(pair, core)], node_dev)
        total = total + dot(pick, loads[k][:bnd, :])
    sum_ref[...] = total


def collect_body(pairs, boundary_ref, sum_ref, kept_ref, node_grad_ref):
    node_dev = sum_ref.shape[0]
    bnd = boundary_ref.shape[2]
    core = core_index()
    total = sum_ref[...]
    for k, pair in enumerate(pairs):
        pick = one_hot_columns(boundary_ref[level_of(pair, 1 - core)], node_dev)
        total = total + dot(pick, kept_ref[k * bnd : (k + 1) * bnd, :])
    node_grad_ref[...] = total.astype(bf16)


def normalize_body(total_ref, out_ref):
    total = total_ref[...].astype(f32)
    mean = jnp.sum(total * total) / total.size
    out_ref[...] = total * lax.rsqrt(jnp.full((1, total.shape[1]), mean + epsilon, f32))


def sum_and_repeat_body(parts_ref, out_ref):
    total = parts_ref[0].astype(f32)
    for part in range(1, parts_ref.shape[0]):
        total = total + parts_ref[part].astype(f32)
    out_ref[...] = jnp.broadcast_to(total.astype(out_ref.dtype)[None], out_ref.shape)


def bit_groups(devices, bits):
    mask = sum(1 << b for b in bits)
    groups = {}
    for i in range(devices):
        groups.setdefault(i & ~mask, []).append(i)
    return list(groups.values())


def exchange(x, groups):
    return lax.all_to_all(x, "dom", 0, 0, axis_index_groups=groups, tiled=True)


def level_pairs(levels):
    pairs = []
    for top in range(levels - 1, 1, -2):
        pairs.append((top, top - 1) if not pairs else (top - 1, top))
    return pairs


def per_device(features, w_self, w_neigh, neighbors, degree, boundary, upstream):
    devices = lax.axis_size("dom")
    levels = devices.bit_length() - 1
    pairs = level_pairs(levels)
    node_dev, width = features.shape
    boundary_rows = boundary.transpose(1, 0, 2)
    bnd = boundary_rows.shape[2]
    rows = node_dev + levels * bnd
    block = (node_dev, width)
    own_shape = shape((len(pairs) * bnd, width), bf16)
    lent_shape = shape(((len(pairs) + 1) * bnd, width), bf16)
    load_shape = shape((2 * bnd, width), bf16)
    near = bit_groups(devices, range(FAST_BITS))
    far = bit_groups(devices, range(FAST_BITS, levels))
    far = [group[len(group) // 2 :] + group[: len(group) // 2] for group in far]
    near = [group[NEAR_FIRST:] + group[:NEAR_FIRST] for group in near]
    piece = 2 * width // len(near[0])
    small = (10**8, 10**6)

    def other_core(x):
        return lax.ppermute(x, "dom", [(i, i ^ 1) for i in range(devices)])

    def across(loads, taken):
        return [
            lax.ppermute(x, "dom", [(i, i ^ 1 << pair[i % 2]) for i in range(devices)])
            for x, pair in zip(loads, taken)
        ]

    def with_pairs(body):
        return lambda *refs: body(pairs, *refs)

    def loaded(own, borrowed, first, last, skip=0):
        return call(
            lambda *refs: load_body(first, skip, *refs),
            [load_shape] * (last - first),
            small,
            own,
            borrowed,
        )

    own, lent = call(
        with_pairs(send_body), [own_shape, lent_shape], (10**9, 10**6), boundary_rows, features
    )
    borrowed = other_core(lent)
    loads = loaded(own, borrowed, 0, len(pairs), skip=1)
    degree_row = degree.reshape(1, node_dev)
    counts = call(
        count_body,
        shape((rows, node_dev), bf16),
        (2 * 10**9, 2 * 10**6),
        neighbors.T,
        degree_row,
        after=(loads[-1],),
    )
    loads = across(loads, pairs)
    kept = other_core(call(unload_body, own_shape, small, *loads, after=(counts,)))
    summed, own_part = call(
        with_pairs(gather_early_body),
        [shape(block, f32)] * 2,
        (10**9, 3 * 10**6),
        counts,
        features,
        w_self,
        borrowed,
        *loads,
    )
    hidden, stacked, pre_grad, share = call(
        with_pairs(layer_body),
        [
            shape(block, bf16),
            shape((2 * width, width), bf16),
            shape(block, bf16),
            shape(block, bf16),
        ],
        (2 * 10**9, 5 * 10**6),
        counts,
        summed,
        own_part,
        kept,
        features,
        degree_row,
        upstream,
        w_neigh,
    )

    parts = exchange(stacked.reshape(len(near[0]), piece, width), near)
    split = len(pairs) // 2
    local, own, lent_a, lent_b = call(
        with_pairs(spread_body),
        [
            shape(block, f32),
            own_shape,
            shape((split * bnd, width), bf16),
            shape(((len(pairs) - split + 1) * bnd, width), bf16),
        ],
        small,
        counts,
        pre_grad,
        share,
        w_self,
    )
    borrowed_a, borrowed_b = other_core(lent_a), other_core(lent_b)
    partial = call(
        sum_and_repeat_body,
        shape((len(far[0]), piece, width), bf16),
        small,
        parts,
        after=(borrowed_a, borrowed_b),
    )
    parts = exchange(partial, far)
    loads = loaded(own, borrowed_a, 0, split) + loaded(own, borrowed_b, split, len(pairs))
    loads = across(loads, pairs)
    total = call(sum_and_repeat_body, shape((len(near[0]), piece, width), bf16), small, parts)
    gathered = exchange(total, near).reshape(2 * width, width)
    kept = other_core(call(unload_body, own_shape, small, *loads, after=(total,)))
    early = call(
        with_pairs(collect_early_body),
        shape(block, f32),
        (10**9, 10**6),
        boundary_rows,
        local,
        borrowed_b,
        *loads,
    )
    node_grad = call(
        with_pairs(collect_body), shape(block, bf16), (10**9, 10**6), boundary_rows, early, kept
    )
    weight_step = call(normalize_body, shape(gathered.shape, f32), small, gathered)
    return (hidden, node_grad, weight_step)


def solution(mesh):
    return jax.shard_map(
        per_device,
        mesh=mesh,
        in_specs=(
            P("dom", None),
            P(),
            P(),
            P("dom", None),
            P("dom"),
            P("dom", None, None),
            P("dom", None),
        ),
        out_specs=(P("dom", None), P("dom", None), P()),
        check_vma=False,
    )
```

```python
import jax
import jax.numpy as jnp
from jax import lax
from jax.experimental import pallas as pl
from jax.experimental.pallas import tpu as pltpu
from jax.sharding import PartitionSpec as P

epsilon = 1e-06
f32 = jnp.float32
bf16 = jnp.bfloat16
FAST_BITS = 5
NEAR_FIRST = 21
VMEM_LIMIT = 16 * 1024 * 1024
TRANSPOSED_LHS = (((0,), (0,)), ((), ()))
TRANSPOSED_RHS = (((1,), (1,)), ((), ()))


def dot(a, b, dims=(((1,), (0,)), ((), ()))):
    return lax.dot_general(a, b, dims, preferred_element_type=f32)


def call(body, outs, cost, *args, after=(), scratch=()):
    flops, moved = cost
    reads, waits = len(args), len(after)
    return pl.pallas_call(
        lambda *refs: body(*refs[:reads], *refs[reads + waits :]),
        out_shape=outs,
        in_specs=[pl.BlockSpec(memory_space=pltpu.VMEM)] * reads
        + [pl.BlockSpec(memory_space=pl.ANY)] * waits,
        scratch_shapes=scratch,
        compiler_params=pltpu.CompilerParams(vmem_limit_bytes=VMEM_LIMIT),
        cost_estimate=pl.CostEstimate(flops=flops, bytes_accessed=moved, transcendentals=0),
    )(*args, *after)


def shape(dims, dtype):
    return jax.ShapeDtypeStruct(dims, dtype)


def one_hot_columns(rows, node_dev):
    k = rows.shape[1]
    ids = lax.broadcasted_iota(jnp.int32, (node_dev, k), 0)
    return jnp.where(ids == rows, f32(1.0), f32(0.0)).astype(bf16)


def core_index():
    return lax.rem(lax.axis_index("dom"), 2)


def level_of(pair, core):
    return jnp.where(core == 0, pair[0], pair[1])


def send_body(pairs, boundary_ref, features_ref, own_ref, lent_ref):
    node_dev = features_ref.shape[0]
    bnd = boundary_ref.shape[2]
    core = core_index()
    features = features_ref[...]

    def rows_of(level):
        pick = one_hot_columns(boundary_ref[level], node_dev)
        return dot(pick, features, TRANSPOSED_LHS).astype(bf16)

    lent_ref[:bnd, :] = rows_of(0)
    for k, pair in enumerate(pairs):
        lent_ref[(k + 1) * bnd : (k + 2) * bnd, :] = rows_of(level_of(pair, 1 - core))
        own_ref[k * bnd : (k + 1) * bnd, :] = rows_of(level_of(pair, core))


def load_body(first, skip, own_ref, borrowed_ref, *load_refs):
    bnd = load_refs[0].shape[0] // 2
    for k, load_ref in enumerate(load_refs):
        load_ref[:bnd, :] = own_ref[(k + first) * bnd : (k + first + 1) * bnd, :]
        load_ref[bnd:, :] = borrowed_ref[(k + skip) * bnd : (k + skip + 1) * bnd, :]


def unload_body(*refs):
    load_refs, lent_ref = refs[:-1], refs[-1]
    bnd = load_refs[0].shape[0] // 2
    for k, load_ref in enumerate(load_refs):
        lent_ref[k * bnd : (k + 1) * bnd, :] = load_ref[bnd:, :]


def count_body(neighbors_ref, degree_ref, counts_ref):
    slots, node_dev = neighbors_ref.shape
    degree = degree_ref[...]
    live = [
        jnp.where(degree > slot, neighbors_ref[slot : slot + 1, :], -1) for slot in range(slots)
    ]
    tile, step = 128, 16
    ids = lax.broadcasted_iota(jnp.int32, (step, node_dev), 0)

    def block(at, carry):
        start = pl.multiple_of(at * tile, tile)
        near = [
            jnp.broadcast_to(row - start, (step, node_dev)).astype(f32).astype(bf16) for row in live
        ]
        for part in range(tile // step):
            here = (ids + part * step).astype(f32).astype(bf16)
            total = jnp.zeros((step, node_dev), bf16)
            for row in near:
                total = total + jnp.where(here == row, bf16(1.0), bf16(0.0))
            counts_ref[pl.ds(start + part * step, step), :] = total
        return carry

    lax.fori_loop(0, counts_ref.shape[0] // tile, block, 0)


def gather_early_body(pairs, counts_ref, features_ref, w_self_ref, borrowed_ref, *refs):
    loads, summed_ref, own_part_ref = refs[:-2], refs[-2], refs[-1]
    node_dev = features_ref.shape[0]
    bnd = borrowed_ref.shape[0] // (len(pairs) + 1)
    core = core_index()
    features = features_ref[...]
    own_part_ref[...] = dot(features, w_self_ref[...])
    summed = dot(counts_ref[:node_dev, :], features, TRANSPOSED_LHS)
    summed = summed + dot(
        counts_ref[node_dev : node_dev + bnd, :], borrowed_ref[:bnd, :], TRANSPOSED_LHS
    )
    for k, pair in enumerate(pairs):
        rows = level_rows(node_dev, bnd, level_of(pair, core))
        summed = summed + dot(counts_ref[rows, :], loads[k][:bnd, :], TRANSPOSED_LHS)
    summed_ref[...] = summed


def level_rows(node_dev, bnd, level):
    return pl.ds(pl.multiple_of(node_dev + level * bnd, bnd), bnd)


def layer_body(
    pairs,
    counts_ref,
    summed_ref,
    own_part_ref,
    kept_ref,
    features_ref,
    degree_ref,
    upstream_ref,
    w_neigh_ref,
    hidden_ref,
    stacked_ref,
    pre_grad_ref,
    share_ref,
):
    node_dev, width = features_ref.shape
    bnd = kept_ref.shape[0] // len(pairs)
    core = core_index()
    degree = degree_ref[...].astype(f32)
    degree = jnp.transpose(jnp.broadcast_to(degree, (128, node_dev)))
    degree = jnp.concatenate([degree] * (width // 128), axis=1)
    summed = summed_ref[...]
    for k, pair in enumerate(pairs):
        rows = level_rows(node_dev, bnd, level_of(pair, 1 - core))
        kept = kept_ref[k * bnd : (k + 1) * bnd, :]
        summed = summed + dot(counts_ref[rows, :], kept, TRANSPOSED_LHS)
    agg = (summed / degree).astype(bf16)
    pre_sum = own_part_ref[...] + dot(agg, w_neigh_ref[...])
    sigmoid_pre = jax.nn.sigmoid(pre_sum)
    hidden_ref[...] = (pre_sum * sigmoid_pre).astype(bf16)
    pre_grad = (
        upstream_ref[...].astype(f32) * sigmoid_pre * (1.0 + pre_sum * (1.0 - sigmoid_pre))
    ).astype(bf16)
    stacked_ref[:width, :] = dot(features_ref[...], pre_grad, TRANSPOSED_LHS).astype(bf16)
    stacked_ref[width:, :] = dot(agg, pre_grad, TRANSPOSED_LHS).astype(bf16)
    share = (dot(pre_grad, w_neigh_ref[...], TRANSPOSED_RHS) / degree).astype(bf16)
    pre_grad_ref[...] = pre_grad
    share_ref[...] = share


def spread_body(
    pairs, counts_ref, pre_grad_ref, share_ref, w_self_ref, local_ref, own_ref, lent_a_ref, lent_b_ref
):
    node_dev = pre_grad_ref.shape[0]
    bnd = own_ref.shape[0] // len(pairs)
    core = core_index()
    pre_grad, share = pre_grad_ref[...], share_ref[...]
    split = lent_a_ref.shape[0] // bnd
    for k, pair in enumerate(pairs):
        rows = level_rows(node_dev, bnd, level_of(pair, 1 - core))
        lent_ref, at = (lent_a_ref, k) if k < split else (lent_b_ref, k - split)
        lent_ref[at * bnd : (at + 1) * bnd, :] = dot(counts_ref[rows, :], share).astype(bf16)
        rows = level_rows(node_dev, bnd, level_of(pair, core))
        own_ref[k * bnd : (k + 1) * bnd, :] = dot(counts_ref[rows, :], share).astype(bf16)
    lent_b_ref[(len(pairs) - split) * bnd :, :] = dot(
        counts_ref[node_dev : node_dev + bnd, :], share
    ).astype(bf16)
    local_ref[...] = dot(pre_grad, w_self_ref[...], TRANSPOSED_RHS) + dot(
        counts_ref[:node_dev, :], share
    )


def collect_early_body(pairs, boundary_ref, local_ref, borrowed_ref, *refs):
    loads, sum_ref = refs[:-1], refs[-1]
    node_dev = local_ref.shape[0]
    bnd = boundary_ref.shape[2]
    core = core_index()
    pick = one_hot_columns(boundary_ref[0], node_dev)
    total = local_ref[...] + dot(pick, borrowed_ref[borrowed_ref.shape[0] - bnd :, :])
    for k, pair in enumerate(pairs):
        pick = one_hot_columns(boundary_ref[level_of(pair, core)], node_dev)
        total = total + dot(pick, loads[k][:bnd, :])
    sum_ref[...] = total


def collect_body(pairs, boundary_ref, sum_ref, kept_ref, node_grad_ref):
    node_dev = sum_ref.shape[0]
    bnd = boundary_ref.shape[2]
    core = core_index()
    total = sum_ref[...]
    for k, pair in enumerate(pairs):
        pick = one_hot_columns(boundary_ref[level_of(pair, 1 - core)], node_dev)
        total = total + dot(pick, kept_ref[k * bnd : (k + 1) * bnd, :])
    node_grad_ref[...] = total.astype(bf16)


def normalize_body(total_ref, out_ref):
    total = total_ref[...].astype(f32)
    mean = jnp.sum(total * total) / total.size
    out_ref[...] = total * lax.rsqrt(jnp.full((1, total.shape[1]), mean + epsilon, f32))


def sum_and_repeat_body(parts_ref, out_ref):
    total = parts_ref[0].astype(f32)
    for part in range(1, parts_ref.shape[0]):
        total = total + parts_ref[part].astype(f32)
    out_ref[...] = jnp.broadcast_to(total.astype(out_ref.dtype)[None], out_ref.shape)


def bit_groups(devices, bits):
    mask = sum(1 << b for b in bits)
    groups = {}
    for i in range(devices):
        groups.setdefault(i & ~mask, []).append(i)
    return list(groups.values())


def exchange(x, groups):
    return lax.all_to_all(x, "dom", 0, 0, axis_index_groups=groups, tiled=True)


def level_pairs(levels):
    pairs = []
    for top in range(levels - 1, 1, -2):
        pairs.append((top, top - 1) if not pairs else (top - 1, top))
    return pairs


def per_device(features, w_self, w_neigh, neighbors, degree, boundary, upstream):
    devices = lax.axis_size("dom")
    levels = devices.bit_length() - 1
    pairs = level_pairs(levels)
    node_dev, width = features.shape
    boundary_rows = boundary.transpose(1, 0, 2)
    bnd = boundary_rows.shape[2]
    rows = node_dev + levels * bnd
    block = (node_dev, width)
    own_shape = shape((len(pairs) * bnd, width), bf16)
    lent_shape = shape(((len(pairs) + 1) * bnd, width), bf16)
    load_shape = shape((2 * bnd, width), bf16)
    near = bit_groups(devices, range(FAST_BITS))
    far = bit_groups(devices, range(FAST_BITS, levels))
    far = [group[len(group) // 2 :] + group[: len(group) // 2] for group in far]
    near = [group[NEAR_FIRST:] + group[:NEAR_FIRST] for group in near]
    piece = 2 * width // len(near[0])
    small = (10**8, 10**6)

    def other_core(x):
        return lax.ppermute(x, "dom", [(i, i ^ 1) for i in range(devices)])

    def across(loads, taken):
        return [
            lax.ppermute(x, "dom", [(i, i ^ 1 << pair[i % 2]) for i in range(devices)])
            for x, pair in zip(loads, taken)
        ]

    def with_pairs(body):
        return lambda *refs: body(pairs, *refs)

    def loaded(own, borrowed, first, last, skip=0):
        return call(
            lambda *refs: load_body(first, skip, *refs),
            [load_shape] * (last - first),
            small,
            own,
            borrowed,
        )

    own, lent = call(
        with_pairs(send_body), [own_shape, lent_shape], (10**9, 10**6), boundary_rows, features
    )
    borrowed = other_core(lent)
    loads = loaded(own, borrowed, 0, len(pairs), skip=1)
    degree_row = degree.reshape(1, node_dev)
    counts = call(
        count_body,
        shape((rows, node_dev), bf16),
        (2 * 10**9, 2 * 10**6),
        neighbors.T,
        degree_row,
        after=(loads[-1],),
    )
    loads = across(loads, pairs)
    kept = other_core(call(unload_body, own_shape, small, *loads, after=(counts,)))
    summed, own_part = call(
        with_pairs(gather_early_body),
        [shape(block, f32)] * 2,
        (10**9, 3 * 10**6),
        counts,
        features,
        w_self,
        borrowed,
        *loads,
    )
    hidden, stacked, pre_grad, share = call(
        with_pairs(layer_body),
        [
            shape(block, bf16),
            shape((2 * width, width), bf16),
            shape(block, bf16),
            shape(block, bf16),
        ],
        (2 * 10**9, 5 * 10**6),
        counts,
        summed,
        own_part,
        kept,
        features,
        degree_row,
        upstream,
        w_neigh,
    )

    parts = exchange(stacked.reshape(len(near[0]), piece, width), near)
    split = len(pairs) // 2
    local, own, lent_a, lent_b = call(
        with_pairs(spread_body),
        [
            shape(block, f32),
            own_shape,
            shape((split * bnd, width), bf16),
            shape(((len(pairs) - split + 1) * bnd, width), bf16),
        ],
        small,
        counts,
        pre_grad,
        share,
        w_self,
    )
    borrowed_a, borrowed_b = other_core(lent_a), other_core(lent_b)
    partial = call(
        sum_and_repeat_body,
        shape((len(far[0]), piece, width), bf16),
        small,
        parts,
        after=(borrowed_a, borrowed_b),
    )
    parts = exchange(partial, far)
    loads = loaded(own, borrowed_a, 0, split) + loaded(own, borrowed_b, split, len(pairs))
    loads = across(loads, pairs)
    total = call(sum_and_repeat_body, shape((len(near[0]), piece, width), bf16), small, parts)
    gathered = exchange(total, near).reshape(2 * width, width)
    kept = other_core(call(unload_body, own_shape, small, *loads, after=(total,)))
    early = call(
        with_pairs(collect_early_body),
        shape(block, f32),
        (10**9, 10**6),
        boundary_rows,
        local,
        borrowed_b,
        *loads,
    )
    node_grad = call(
        with_pairs(collect_body), shape(block, bf16), (10**9, 10**6), boundary_rows, early, kept
    )
    weight_step = call(normalize_body, shape(gathered.shape, f32), small, gathered)
    return (hidden, node_grad, weight_step)


def solution(mesh):
    return jax.shard_map(
        per_device,
        mesh=mesh,
        in_specs=(
            P("dom", None),
            P(),
            P(),
            P("dom", None),
            P("dom"),
            P("dom", None, None),
            P("dom", None),
        ),
        out_specs=(P("dom", None), P("dom", None), P()),
        check_vma=False,
    )
```

```python
import jax
import jax.numpy as jnp
from jax import lax
from jax.experimental import pallas as pl
from jax.experimental.pallas import tpu as pltpu
from jax.sharding import PartitionSpec as P

epsilon = 1e-06
f32 = jnp.float32
bf16 = jnp.bfloat16
FAST_BITS = 5
NEAR_FIRST = 21
VMEM_LIMIT = 16 * 1024 * 1024
TRANSPOSED_LHS = (((0,), (0,)), ((), ()))
TRANSPOSED_RHS = (((1,), (1,)), ((), ()))


def dot(a, b, dims=(((1,), (0,)), ((), ()))):
    return lax.dot_general(a, b, dims, preferred_element_type=f32)


def call(body, outs, cost, *args, after=(), scratch=()):
    flops, moved = cost
    reads, waits = len(args), len(after)
    return pl.pallas_call(
        lambda *refs: body(*refs[:reads], *refs[reads + waits :]),
        out_shape=outs,
        in_specs=[pl.BlockSpec(memory_space=pltpu.VMEM)] * reads
        + [pl.BlockSpec(memory_space=pl.ANY)] * waits,
        scratch_shapes=scratch,
        compiler_params=pltpu.CompilerParams(vmem_limit_bytes=VMEM_LIMIT),
        cost_estimate=pl.CostEstimate(flops=flops, bytes_accessed=moved, transcendentals=0),
    )(*args, *after)


def shape(dims, dtype):
    return jax.ShapeDtypeStruct(dims, dtype)


def one_hot_columns(rows, node_dev):
    k = rows.shape[1]
    ids = lax.broadcasted_iota(jnp.int32, (node_dev, k), 0)
    return jnp.where(ids == rows, f32(1.0), f32(0.0)).astype(bf16)


def core_index():
    return lax.rem(lax.axis_index("dom"), 2)


def level_of(pair, core):
    return jnp.where(core == 0, pair[0], pair[1])


def send_body(pairs, boundary_ref, features_ref, own_ref, lent_ref):
    node_dev = features_ref.shape[0]
    bnd = boundary_ref.shape[2]
    core = core_index()
    features = features_ref[...]

    def rows_of(level):
        pick = one_hot_columns(boundary_ref[level], node_dev)
        return dot(pick, features, TRANSPOSED_LHS).astype(bf16)

    lent_ref[:bnd, :] = rows_of(0)
    for k, pair in enumerate(pairs):
        lent_ref[(k + 1) * bnd : (k + 2) * bnd, :] = rows_of(level_of(pair, 1 - core))
        own_ref[k * bnd : (k + 1) * bnd, :] = rows_of(level_of(pair, core))


def load_body(first, skip, own_ref, borrowed_ref, *load_refs):
    bnd = load_refs[0].shape[0] // 2
    for k, load_ref in enumerate(load_refs):
        load_ref[:bnd, :] = own_ref[(k + first) * bnd : (k + first + 1) * bnd, :]
        load_ref[bnd:, :] = borrowed_ref[(k + skip) * bnd : (k + skip + 1) * bnd, :]


def unload_body(*refs):
    load_refs, lent_ref = refs[:-1], refs[-1]
    bnd = load_refs[0].shape[0] // 2
    for k, load_ref in enumerate(load_refs):
        lent_ref[k * bnd : (k + 1) * bnd, :] = load_ref[bnd:, :]


def count_body(neighbors_ref, degree_ref, counts_ref):
    slots, node_dev = neighbors_ref.shape
    degree = degree_ref[...]
    live = [
        jnp.where(degree > slot, neighbors_ref[slot : slot + 1, :], -1) for slot in range(slots)
    ]
    tile, step = 128, 16
    ids = lax.broadcasted_iota(jnp.int32, (step, node_dev), 0)

    def block(at, carry):
        start = pl.multiple_of(at * tile, tile)
        near = [
            jnp.broadcast_to(row - start, (step, node_dev)).astype(f32).astype(bf16) for row in live
        ]
        for part in range(tile // step):
            here = (ids + part * step).astype(f32).astype(bf16)
            total = jnp.zeros((step, node_dev), bf16)
            for row in near:
                total = total + jnp.where(here == row, bf16(1.0), bf16(0.0))
            counts_ref[pl.ds(start + part * step, step), :] = total
        return carry

    lax.fori_loop(0, counts_ref.shape[0] // tile, block, 0)


def gather_early_body(pairs, counts_ref, features_ref, w_self_ref, borrowed_ref, *refs):
    loads, summed_ref, own_part_ref = refs[:-2], refs[-2], refs[-1]
    node_dev = features_ref.shape[0]
    bnd = borrowed_ref.shape[0] // (len(pairs) + 1)
    core = core_index()
    features = features_ref[...]
    own_part_ref[...] = dot(features, w_self_ref[...])
    summed = dot(counts_ref[:node_dev, :], features, TRANSPOSED_LHS)
    summed = summed + dot(
        counts_ref[node_dev : node_dev + bnd, :], borrowed_ref[:bnd, :], TRANSPOSED_LHS
    )
    for k, pair in enumerate(pairs):
        rows = level_rows(node_dev, bnd, level_of(pair, core))
        summed = summed + dot(counts_ref[rows, :], loads[k][:bnd, :], TRANSPOSED_LHS)
    summed_ref[...] = summed


def level_rows(node_dev, bnd, level):
    return pl.ds(pl.multiple_of(node_dev + level * bnd, bnd), bnd)


def layer_body(
    pairs,
    counts_ref,
    summed_ref,
    own_part_ref,
    kept_ref,
    features_ref,
    degree_ref,
    upstream_ref,
    w_neigh_ref,
    hidden_ref,
    stacked_ref,
    pre_grad_ref,
    share_ref,
):
    node_dev, width = features_ref.shape
    bnd = kept_ref.shape[0] // len(pairs)
    core = core_index()
    degree = degree_ref[...].astype(f32)
    degree = jnp.transpose(jnp.broadcast_to(degree, (128, node_dev)))
    degree = jnp.concatenate([degree] * (width // 128), axis=1)
    summed = summed_ref[...]
    for k, pair in enumerate(pairs):
        rows = level_rows(node_dev, bnd, level_of(pair, 1 - core))
        kept = kept_ref[k * bnd : (k + 1) * bnd, :]
        summed = summed + dot(counts_ref[rows, :], kept, TRANSPOSED_LHS)
    agg = (summed / degree).astype(bf16)
    pre_sum = own_part_ref[...] + dot(agg, w_neigh_ref[...])
    sigmoid_pre = jax.nn.sigmoid(pre_sum)
    hidden_ref[...] = (pre_sum * sigmoid_pre).astype(bf16)
    pre_grad = (
        upstream_ref[...].astype(f32) * sigmoid_pre * (1.0 + pre_sum * (1.0 - sigmoid_pre))
    ).astype(bf16)
    stacked_ref[:width, :] = dot(features_ref[...], pre_grad, TRANSPOSED_LHS).astype(bf16)
    stacked_ref[width:, :] = dot(agg, pre_grad, TRANSPOSED_LHS).astype(bf16)
    share = (dot(pre_grad, w_neigh_ref[...], TRANSPOSED_RHS) / degree).astype(bf16)
    pre_grad_ref[...] = pre_grad
    share_ref[...] = share


def spread_body(
    pairs, counts_ref, pre_grad_ref, share_ref, w_self_ref, local_ref, own_ref, lent_a_ref, lent_b_ref
):
    node_dev = pre_grad_ref.shape[0]
    bnd = own_ref.shape[0] // len(pairs)
    core = core_index()
    pre_grad, share = pre_grad_ref[...], share_ref[...]
    split = lent_a_ref.shape[0] // bnd
    for k, pair in enumerate(pairs):
        rows = level_rows(node_dev, bnd, level_of(pair, 1 - core))
        lent_ref, at = (lent_a_ref, k) if k < split else (lent_b_ref, k - split)
        lent_ref[at * bnd : (at + 1) * bnd, :] = dot(counts_ref[rows, :], share).astype(bf16)
        rows = level_rows(node_dev, bnd, level_of(pair, core))
        own_ref[k * bnd : (k + 1) * bnd, :] = dot(counts_ref[rows, :], share).astype(bf16)
    lent_b_ref[(len(pairs) - split) * bnd :, :] = dot(
        counts_ref[node_dev : node_dev + bnd, :], share
    ).astype(bf16)
    local_ref[...] = dot(pre_grad, w_self_ref[...], TRANSPOSED_RHS) + dot(
        counts_ref[:node_dev, :], share
    )


def collect_early_body(pairs, boundary_ref, local_ref, borrowed_ref, *refs):
    loads, sum_ref = refs[:-1], refs[-1]
    node_dev = local_ref.shape[0]
    bnd = boundary_ref.shape[2]
    core = core_index()
    pick = one_hot_columns(boundary_ref[0], node_dev)
    total = local_ref[...] + dot(pick, borrowed_ref[borrowed_ref.shape[0] - bnd :, :])
    for k, pair in enumerate(pairs):
        pick = one_hot_columns(boundary_ref[level_of(pair, core)], node_dev)
        total = total + dot(pick, loads[k][:bnd, :])
    sum_ref[...] = total


def collect_body(pairs, boundary_ref, sum_ref, kept_ref, node_grad_ref):
    node_dev = sum_ref.shape[0]
    bnd = boundary_ref.shape[2]
    core = core_index()
    total = sum_ref[...]
    for k, pair in enumerate(pairs):
        pick = one_hot_columns(boundary_ref[level_of(pair, 1 - core)], node_dev)
        total = total + dot(pick, kept_ref[k * bnd : (k + 1) * bnd, :])
    node_grad_ref[...] = total.astype(bf16)


def normalize_body(total_ref, out_ref):
    total = total_ref[...].astype(f32)
    mean = jnp.sum(total * total) / total.size
    out_ref[...] = total * lax.rsqrt(jnp.full((1, total.shape[1]), mean + epsilon, f32))


def sum_and_repeat_body(parts_ref, out_ref):
    total = parts_ref[0].astype(f32)
    for part in range(1, parts_ref.shape[0]):
        total = total + parts_ref[part].astype(f32)
    out_ref[...] = jnp.broadcast_to(total.astype(out_ref.dtype)[None], out_ref.shape)


def bit_groups(devices, bits):
    mask = sum(1 << b for b in bits)
    groups = {}
    for i in range(devices):
        groups.setdefault(i & ~mask, []).append(i)
    return list(groups.values())


def exchange(x, groups):
    return lax.all_to_all(x, "dom", 0, 0, axis_index_groups=groups, tiled=True)


def level_pairs(levels):
    pairs = []
    for top in range(levels - 1, 1, -2):
        pairs.append((top, top - 1) if not pairs else (top - 1, top))
    return pairs[: len(pairs) // 2] + pairs[len(pairs) // 2 :][::-1]


def per_device(features, w_self, w_neigh, neighbors, degree, boundary, upstream):
    devices = lax.axis_size("dom")
    levels = devices.bit_length() - 1
    pairs = level_pairs(levels)
    node_dev, width = features.shape
    boundary_rows = boundary.transpose(1, 0, 2)
    bnd = boundary_rows.shape[2]
    rows = node_dev + levels * bnd
    block = (node_dev, width)
    own_shape = shape((len(pairs) * bnd, width), bf16)
    lent_shape = shape(((len(pairs) + 1) * bnd, width), bf16)
    load_shape = shape((2 * bnd, width), bf16)
    near = bit_groups(devices, range(FAST_BITS))
    far = bit_groups(devices, range(FAST_BITS, levels))
    far = [group[len(group) // 2 :] + group[: len(group) // 2] for group in far]
    near = [group[NEAR_FIRST:] + group[:NEAR_FIRST] for group in near]
    piece = 2 * width // len(near[0])
    small = (10**8, 10**6)

    def other_core(x):
        return lax.ppermute(x, "dom", [(i, i ^ 1) for i in range(devices)])

    def across(loads, taken):
        return [
            lax.ppermute(x, "dom", [(i, i ^ 1 << pair[i % 2]) for i in range(devices)])
            for x, pair in zip(loads, taken)
        ]

    def with_pairs(body):
        return lambda *refs: body(pairs, *refs)

    def loaded(own, borrowed, first, last, skip=0):
        return call(
            lambda *refs: load_body(first, skip, *refs),
            [load_shape] * (last - first),
            small,
            own,
            borrowed,
        )

    own, lent = call(
        with_pairs(send_body), [own_shape, lent_shape], (10**9, 10**6), boundary_rows, features
    )
    borrowed = other_core(lent)
    loads = loaded(own, borrowed, 0, len(pairs), skip=1)
    degree_row = degree.reshape(1, node_dev)
    counts = call(
        count_body,
        shape((rows, node_dev), bf16),
        (2 * 10**9, 2 * 10**6),
        neighbors.T,
        degree_row,
        after=(loads[-1],),
    )
    loads = across(loads, pairs)
    kept = other_core(call(unload_body, own_shape, small, *loads, after=(counts,)))
    summed, own_part = call(
        with_pairs(gather_early_body),
        [shape(block, f32)] * 2,
        (10**9, 3 * 10**6),
        counts,
        features,
        w_self,
        borrowed,
        *loads,
    )
    hidden, stacked, pre_grad, share = call(
        with_pairs(layer_body),
        [
            shape(block, bf16),
            shape((2 * width, width), bf16),
            shape(block, bf16),
            shape(block, bf16),
        ],
        (2 * 10**9, 5 * 10**6),
        counts,
        summed,
        own_part,
        kept,
        features,
        degree_row,
        upstream,
        w_neigh,
    )

    parts = exchange(stacked.reshape(len(near[0]), piece, width), near)
    split = len(pairs) // 2
    local, own, lent_a, lent_b = call(
        with_pairs(spread_body),
        [
            shape(block, f32),
            own_shape,
            shape((split * bnd, width), bf16),
            shape(((len(pairs) - split + 1) * bnd, width), bf16),
        ],
        small,
        counts,
        pre_grad,
        share,
        w_self,
    )
    borrowed_a, borrowed_b = other_core(lent_a), other_core(lent_b)
    partial = call(
        sum_and_repeat_body,
        shape((len(far[0]), piece, width), bf16),
        small,
        parts,
        after=(borrowed_a, borrowed_b),
    )
    parts = exchange(partial, far)
    loads = loaded(own, borrowed_a, 0, split) + loaded(own, borrowed_b, split, len(pairs))
    loads = across(loads, pairs)
    total = call(sum_and_repeat_body, shape((len(near[0]), piece, width), bf16), small, parts)
    gathered = exchange(total, near).reshape(2 * width, width)
    kept = other_core(call(unload_body, own_shape, small, *loads, after=(total,)))
    early = call(
        with_pairs(collect_early_body),
        shape(block, f32),
        (10**9, 10**6),
        boundary_rows,
        local,
        borrowed_b,
        *loads,
    )
    node_grad = call(
        with_pairs(collect_body), shape(block, bf16), (10**9, 10**6), boundary_rows, early, kept
    )
    weight_step = call(normalize_body, shape(gathered.shape, f32), small, gathered)
    return (hidden, node_grad, weight_step)


def solution(mesh):
    return jax.shard_map(
        per_device,
        mesh=mesh,
        in_specs=(
            P("dom", None),
            P(),
            P(),
            P("dom", None),
            P("dom"),
            P("dom", None, None),
            P("dom", None),
        ),
        out_specs=(P("dom", None), P("dom", None), P()),
        check_vma=False,
    )
```

```python
import jax
import jax.numpy as jnp
from jax import lax
from jax.experimental import pallas as pl
from jax.experimental.pallas import tpu as pltpu
from jax.sharding import PartitionSpec as P

epsilon = 1e-06
f32 = jnp.float32
bf16 = jnp.bfloat16
FAST_BITS = 5
NEAR_FIRST = 21
FAR_FIRST = 9
VMEM_LIMIT = 16 * 1024 * 1024
TRANSPOSED_LHS = (((0,), (0,)), ((), ()))
TRANSPOSED_RHS = (((1,), (1,)), ((), ()))


def dot(a, b, dims=(((1,), (0,)), ((), ()))):
    return lax.dot_general(a, b, dims, preferred_element_type=f32)


def call(body, outs, cost, *args, after=(), scratch=()):
    flops, moved = cost
    reads, waits = len(args), len(after)
    return pl.pallas_call(
        lambda *refs: body(*refs[:reads], *refs[reads + waits :]),
        out_shape=outs,
        in_specs=[pl.BlockSpec(memory_space=pltpu.VMEM)] * reads
        + [pl.BlockSpec(memory_space=pl.ANY)] * waits,
        scratch_shapes=scratch,
        compiler_params=pltpu.CompilerParams(vmem_limit_bytes=VMEM_LIMIT),
        cost_estimate=pl.CostEstimate(flops=flops, bytes_accessed=moved, transcendentals=0),
    )(*args, *after)


def shape(dims, dtype):
    return jax.ShapeDtypeStruct(dims, dtype)


def one_hot_columns(rows, node_dev):
    k = rows.shape[1]
    ids = lax.broadcasted_iota(jnp.int32, (node_dev, k), 0)
    return jnp.where(ids == rows, f32(1.0), f32(0.0)).astype(bf16)


def core_index():
    return lax.rem(lax.axis_index("dom"), 2)


def level_of(pair, core):
    return jnp.where(core == 0, pair[0], pair[1])


def send_body(pairs, boundary_ref, features_ref, own_ref, lent_ref):
    node_dev = features_ref.shape[0]
    bnd = boundary_ref.shape[2]
    core = core_index()
    features = features_ref[...]

    def rows_of(level):
        pick = one_hot_columns(boundary_ref[level], node_dev)
        return dot(pick, features, TRANSPOSED_LHS).astype(bf16)

    lent_ref[:bnd, :] = rows_of(0)
    for k, pair in enumerate(pairs):
        lent_ref[(k + 1) * bnd : (k + 2) * bnd, :] = rows_of(level_of(pair, 1 - core))
        own_ref[k * bnd : (k + 1) * bnd, :] = rows_of(level_of(pair, core))


def load_body(first, skip, own_ref, borrowed_ref, *load_refs):
    bnd = load_refs[0].shape[0] // 2
    for k, load_ref in enumerate(load_refs):
        load_ref[:bnd, :] = own_ref[(k + first) * bnd : (k + first + 1) * bnd, :]
        load_ref[bnd:, :] = borrowed_ref[(k + skip) * bnd : (k + skip + 1) * bnd, :]


def unload_body(*refs):
    load_refs, lent_ref = refs[:-1], refs[-1]
    bnd = load_refs[0].shape[0] // 2
    for k, load_ref in enumerate(load_refs):
        lent_ref[k * bnd : (k + 1) * bnd, :] = load_ref[bnd:, :]


def count_body(neighbors_ref, degree_ref, counts_ref):
    slots, node_dev = neighbors_ref.shape
    degree = degree_ref[...]
    live = [
        jnp.where(degree > slot, neighbors_ref[slot : slot + 1, :], -1) for slot in range(slots)
    ]
    tile, step = 128, 16
    ids = lax.broadcasted_iota(jnp.int32, (step, node_dev), 0)

    def block(at, carry):
        start = pl.multiple_of(at * tile, tile)
        near = [
            jnp.broadcast_to(row - start, (step, node_dev)).astype(f32).astype(bf16) for row in live
        ]
        for part in range(tile // step):
            here = (ids + part * step).astype(f32).astype(bf16)
            total = jnp.zeros((step, node_dev), bf16)
            for row in near:
                total = total + jnp.where(here == row, bf16(1.0), bf16(0.0))
            counts_ref[pl.ds(start + part * step, step), :] = total
        return carry

    lax.fori_loop(0, counts_ref.shape[0] // tile, block, 0)


def gather_early_body(pairs, counts_ref, features_ref, w_self_ref, borrowed_ref, *refs):
    loads, summed_ref, own_part_ref = refs[:-2], refs[-2], refs[-1]
    node_dev = features_ref.shape[0]
    bnd = borrowed_ref.shape[0] // (len(pairs) + 1)
    core = core_index()
    features = features_ref[...]
    own_part_ref[...] = dot(features, w_self_ref[...])
    summed = dot(counts_ref[:node_dev, :], features, TRANSPOSED_LHS)
    summed = summed + dot(
        counts_ref[node_dev : node_dev + bnd, :], borrowed_ref[:bnd, :], TRANSPOSED_LHS
    )
    for k, pair in enumerate(pairs):
        rows = level_rows(node_dev, bnd, level_of(pair, core))
        summed = summed + dot(counts_ref[rows, :], loads[k][:bnd, :], TRANSPOSED_LHS)
    summed_ref[...] = summed


def level_rows(node_dev, bnd, level):
    return pl.ds(pl.multiple_of(node_dev + level * bnd, bnd), bnd)


def layer_body(
    pairs,
    counts_ref,
    summed_ref,
    own_part_ref,
    kept_ref,
    features_ref,
    degree_ref,
    upstream_ref,
    w_neigh_ref,
    hidden_ref,
    stacked_ref,
    pre_grad_ref,
    share_ref,
):
    node_dev, width = features_ref.shape
    bnd = kept_ref.shape[0] // len(pairs)
    core = core_index()
    degree = degree_ref[...].astype(f32)
    degree = jnp.transpose(jnp.broadcast_to(degree, (128, node_dev)))
    degree = jnp.concatenate([degree] * (width // 128), axis=1)
    summed = summed_ref[...]
    for k, pair in enumerate(pairs):
        rows = level_rows(node_dev, bnd, level_of(pair, 1 - core))
        kept = kept_ref[k * bnd : (k + 1) * bnd, :]
        summed = summed + dot(counts_ref[rows, :], kept, TRANSPOSED_LHS)
    agg = (summed / degree).astype(bf16)
    pre_sum = own_part_ref[...] + dot(agg, w_neigh_ref[...])
    sigmoid_pre = jax.nn.sigmoid(pre_sum)
    hidden_ref[...] = (pre_sum * sigmoid_pre).astype(bf16)
    pre_grad = (
        upstream_ref[...].astype(f32) * sigmoid_pre * (1.0 + pre_sum * (1.0 - sigmoid_pre))
    ).astype(bf16)
    stacked_ref[:width, :] = dot(features_ref[...], pre_grad, TRANSPOSED_LHS).astype(bf16)
    stacked_ref[width:, :] = dot(agg, pre_grad, TRANSPOSED_LHS).astype(bf16)
    share = (dot(pre_grad, w_neigh_ref[...], TRANSPOSED_RHS) / degree).astype(bf16)
    pre_grad_ref[...] = pre_grad
    share_ref[...] = share


def spread_body(
    pairs, counts_ref, pre_grad_ref, share_ref, w_self_ref, local_ref, own_ref, lent_a_ref, lent_b_ref
):
    node_dev = pre_grad_ref.shape[0]
    bnd = own_ref.shape[0] // len(pairs)
    core = core_index()
    pre_grad, share = pre_grad_ref[...], share_ref[...]
    split = lent_a_ref.shape[0] // bnd
    for k, pair in enumerate(pairs):
        rows = level_rows(node_dev, bnd, level_of(pair, 1 - core))
        lent_ref, at = (lent_a_ref, k) if k < split else (lent_b_ref, k - split)
        lent_ref[at * bnd : (at + 1) * bnd, :] = dot(counts_ref[rows, :], share).astype(bf16)
        rows = level_rows(node_dev, bnd, level_of(pair, core))
        own_ref[k * bnd : (k + 1) * bnd, :] = dot(counts_ref[rows, :], share).astype(bf16)
    lent_b_ref[(len(pairs) - split) * bnd :, :] = dot(
        counts_ref[node_dev : node_dev + bnd, :], share
    ).astype(bf16)
    local_ref[...] = dot(pre_grad, w_self_ref[...], TRANSPOSED_RHS) + dot(
        counts_ref[:node_dev, :], share
    )


def collect_early_body(pairs, boundary_ref, local_ref, borrowed_ref, *refs):
    loads, sum_ref = refs[:-1], refs[-1]
    node_dev = local_ref.shape[0]
    bnd = boundary_ref.shape[2]
    core = core_index()
    pick = one_hot_columns(boundary_ref[0], node_dev)
    total = local_ref[...] + dot(pick, borrowed_ref[borrowed_ref.shape[0] - bnd :, :])
    for k, pair in enumerate(pairs):
        pick = one_hot_columns(boundary_ref[level_of(pair, core)], node_dev)
        total = total + dot(pick, loads[k][:bnd, :])
    sum_ref[...] = total


def collect_body(pairs, boundary_ref, sum_ref, kept_ref, node_grad_ref):
    node_dev = sum_ref.shape[0]
    bnd = boundary_ref.shape[2]
    core = core_index()
    total = sum_ref[...]
    for k, pair in enumerate(pairs):
        pick = one_hot_columns(boundary_ref[level_of(pair, 1 - core)], node_dev)
        total = total + dot(pick, kept_ref[k * bnd : (k + 1) * bnd, :])
    node_grad_ref[...] = total.astype(bf16)


def normalize_body(total_ref, out_ref):
    total = total_ref[...].astype(f32)
    mean = jnp.sum(total * total) / total.size
    out_ref[...] = total * lax.rsqrt(jnp.full((1, total.shape[1]), mean + epsilon, f32))


def sum_and_repeat_body(parts_ref, out_ref):
    total = parts_ref[0].astype(f32)
    for part in range(1, parts_ref.shape[0]):
        total = total + parts_ref[part].astype(f32)
    out_ref[...] = jnp.broadcast_to(total.astype(out_ref.dtype)[None], out_ref.shape)


def bit_groups(devices, bits):
    mask = sum(1 << b for b in bits)
    groups = {}
    for i in range(devices):
        groups.setdefault(i & ~mask, []).append(i)
    return list(groups.values())


def exchange(x, groups):
    return lax.all_to_all(x, "dom", 0, 0, axis_index_groups=groups, tiled=True)


def level_pairs(levels):
    pairs = []
    for top in range(levels - 1, 1, -2):
        pairs.append((top, top - 1) if not pairs else (top - 1, top))
    return pairs


def per_device(features, w_self, w_neigh, neighbors, degree, boundary, upstream):
    devices = lax.axis_size("dom")
    levels = devices.bit_length() - 1
    pairs = level_pairs(levels)
    node_dev, width = features.shape
    boundary_rows = boundary.transpose(1, 0, 2)
    bnd = boundary_rows.shape[2]
    rows = node_dev + levels * bnd
    block = (node_dev, width)
    own_shape = shape((len(pairs) * bnd, width), bf16)
    lent_shape = shape(((len(pairs) + 1) * bnd, width), bf16)
    load_shape = shape((2 * bnd, width), bf16)
    near = bit_groups(devices, range(FAST_BITS))
    far = bit_groups(devices, range(FAST_BITS, levels))
    far = [group[FAR_FIRST:] + group[:FAR_FIRST] for group in far]
    near = [group[NEAR_FIRST:] + group[:NEAR_FIRST] for group in near]
    piece = 2 * width // len(near[0])
    small = (10**8, 10**6)

    def other_core(x):
        return lax.ppermute(x, "dom", [(i, i ^ 1) for i in range(devices)])

    def across(loads, taken):
        return [
            lax.ppermute(x, "dom", [(i, i ^ 1 << pair[i % 2]) for i in range(devices)])
            for x, pair in zip(loads, taken)
        ]

    def with_pairs(body):
        return lambda *refs: body(pairs, *refs)

    def loaded(own, borrowed, first, last, skip=0):
        return call(
            lambda *refs: load_body(first, skip, *refs),
            [load_shape] * (last - first),
            small,
            own,
            borrowed,
        )

    own, lent = call(
        with_pairs(send_body), [own_shape, lent_shape], (10**9, 10**6), boundary_rows, features
    )
    borrowed = other_core(lent)
    loads = loaded(own, borrowed, 0, len(pairs), skip=1)
    degree_row = degree.reshape(1, node_dev)
    counts = call(
        count_body,
        shape((rows, node_dev), bf16),
        (2 * 10**9, 2 * 10**6),
        neighbors.T,
        degree_row,
        after=(loads[-1],),
    )
    loads = across(loads, pairs)
    kept = other_core(call(unload_body, own_shape, small, *loads, after=(counts,)))
    summed, own_part = call(
        with_pairs(gather_early_body),
        [shape(block, f32)] * 2,
        (10**9, 3 * 10**6),
        counts,
        features,
        w_self,
        borrowed,
        *loads,
    )
    hidden, stacked, pre_grad, share = call(
        with_pairs(layer_body),
        [
            shape(block, bf16),
            shape((2 * width, width), bf16),
            shape(block, bf16),
            shape(block, bf16),
        ],
        (2 * 10**9, 5 * 10**6),
        counts,
        summed,
        own_part,
        kept,
        features,
        degree_row,
        upstream,
        w_neigh,
    )

    parts = exchange(stacked.reshape(len(near[0]), piece, width), near)
    split = len(pairs) // 2
    local, own, lent_a, lent_b = call(
        with_pairs(spread_body),
        [
            shape(block, f32),
            own_shape,
            shape((split * bnd, width), bf16),
            shape(((len(pairs) - split + 1) * bnd, width), bf16),
        ],
        small,
        counts,
        pre_grad,
        share,
        w_self,
    )
    borrowed_a, borrowed_b = other_core(lent_a), other_core(lent_b)
    partial = call(
        sum_and_repeat_body,
        shape((len(far[0]), piece, width), bf16),
        small,
        parts,
        after=(borrowed_a, borrowed_b),
    )
    parts = exchange(partial, far)
    loads = loaded(own, borrowed_a, 0, split) + loaded(own, borrowed_b, split, len(pairs))
    loads = across(loads, pairs)
    total = call(sum_and_repeat_body, shape((len(near[0]), piece, width), bf16), small, parts)
    gathered = exchange(total, near).reshape(2 * width, width)
    kept = other_core(call(unload_body, own_shape, small, *loads, after=(total,)))
    early = call(
        with_pairs(collect_early_body),
        shape(block, f32),
        (10**9, 10**6),
        boundary_rows,
        local,
        borrowed_b,
        *loads,
    )
    node_grad = call(
        with_pairs(collect_body), shape(block, bf16), (10**9, 10**6), boundary_rows, early, kept
    )
    weight_step = call(normalize_body, shape(gathered.shape, f32), small, gathered)
    return (hidden, node_grad, weight_step)


def solution(mesh):
    return jax.shard_map(
        per_device,
        mesh=mesh,
        in_specs=(
            P("dom", None),
            P(),
            P(),
            P("dom", None),
            P("dom"),
            P("dom", None, None),
            P("dom", None),
        ),
        out_specs=(P("dom", None), P("dom", None), P()),
        check_vma=False,
    )
```
